256 devices in a mesh: grp: 8 (over y, core), dev: 32 (over z, x).
Axes of the slice: x: 4, y: 4, z: 8, core: 2. Of those that a mesh axis runs over, the one named last changes fastest.
Arguments:
- node_feat: bfloat16 [1048576, 256], P(('grp', 'dev')), may hold values from -6 to 6
- coarse_feat: bfloat16 [131072, 256], P(('grp', 'dev')), may hold values from -6 to 6
- cotangent: bfloat16 [1048576, 256], P(('grp', 'dev')), may hold values from -6 to 6
- w_restrict: bfloat16 [256, 256], replicated, may hold values from -0.375 to 0.375
- w_coarse: bfloat16 [256, 256], replicated, may hold values from -0.375 to 0.375
- w_prolong: bfloat16 [256, 256], replicated, may hold values from -0.375 to 0.375
- owner: int32 [1048576], P(('grp', 'dev')), may hold values from 0 to 31, as said below
- slot: int32 [1048576], P(('grp', 'dev')), may hold values from 0 to 255
- recv_row: int32 [2097152], P(('grp', 'dev')), may hold values from 0 to 511
Outputs:
- grad_node: bfloat16 [1048576, 256], P(('grp', 'dev'))
- grad_coarse: bfloat16 [131072, 256], P(('grp', 'dev'))
- grad_wr: float32 [256, 256], replicated
- grad_wc: float32 [256, 256], replicated
- grad_wp: float32 [256, 256], replicated
The draws below stay inside these ranges and needn't reach their ends.
Inputs may be any that keep to these rules, and one draw needn't show every extreme that they name: On each device the pairs (owner, slot) of its fine nodes are distinct, and exactly 256 of its fine nodes name the device's own index along dev.
All inputs are finite; a program needn't handle non-finite values.
Results may differ from the reference program's by a relative error of at most 0.01.
Values may be sent and summed in bfloat16 or wider, within the bound.
A program may use at most 128 MiB of HBM per device.

```python
import jax
import jax.numpy as jnp
from jax import lax

H = 256
N0_DEV = 4096
N1_DEV = 512
CAP = 256
SHARDS = 256
N0 = 1048576
N1 = 131072
SLOTS = 2097152
N_GRP = 8
N_DEV = 32


def layout(key):
    keys = jax.random.split(key, SHARDS)

    def one_device(subkey, device):
        local = device % N_DEV
        first, second = jax.random.split(subkey)
        others = jax.random.permutation(first, (N_DEV - 1) * CAP)[:N0_DEV - CAP].astype(jnp.int32)
        own_owner = jnp.full((CAP,), 0, jnp.int32) + local
        own_slot = jnp.arange(CAP, dtype=jnp.int32)
        far_owner = (local + 1 + others // CAP) % N_DEV
        far_slot = others % CAP
        owners = jnp.concatenate([own_owner, far_owner])
        slots = jnp.concatenate([own_slot, far_slot])
        order = jax.random.permutation(second, N0_DEV).astype(jnp.int32)
        return (owners[order], slots[order])
    owners, slots = jax.vmap(one_device)(keys, jnp.arange(SHARDS, dtype=jnp.int32))
    return (owners.reshape(-1).astype(jnp.int32), slots.reshape(-1).astype(jnp.int32))


def draw_owner(key, part):
    return layout(key)[0]


def draw_slot(key, part):
    return layout(key)[1]


def place_ends(values, stream_key, least, top_value):
    longest = values.shape.index(max(values.shape))
    spots = []
    for shift in (0, 1):
        where = [jax.random.randint(jax.random.fold_in(stream_key, axis), (), 0, length) for axis, length in enumerate(values.shape)]
        where[longest] = (where[longest] + shift) % values.shape[longest]
        spots.append(tuple(where))
    return values.at[spots[0]].set(least).at[spots[1]].set(top_value)


def block_scale(own_key, dims, shards, least, top_value):
    def one(axis_at, parts):
        heights = jax.random.uniform(jax.random.fold_in(jax.random.fold_in(own_key, 6), axis_at), (parts,), jnp.float32, least / len(shards), top_value / len(shards))
        return jnp.repeat(jnp.exp(heights), dims[axis_at] // parts).reshape((-1,) + (1,) * (len(dims) - axis_at - 1))

    loudness = one(*shards[0])
    for cut in shards[1:]:
        loudness = loudness * one(*cut)
    return loudness


def centred(rng, extent, deviation, bound, pieces=(), kind=jnp.bfloat16):
    factor_of = block_scale(rng, extent, pieces, -0.22, 0.18) if pieces else 1.0
    entries = jax.random.normal(rng, extent, jnp.float32) * deviation * factor_of
    return jnp.minimum(jnp.maximum(entries, -bound), bound).astype(kind)


def setup_inputs(seed: int = 0) -> dict:
    key_of = jax.random.split(jax.random.key(seed), 10)
    node_feat = centred(key_of[0], (N0, H), 1.0, 6.0, ((0, 256),))
    coarse_feat = centred(key_of[1], (N1, H), 1.0, 6.0, ((0, 256),))
    cotangent = centred(key_of[2], (N0, H), 1.0, 6.0, ((0, 256),))
    w_restrict = centred(key_of[3], (H, H), H ** -0.5, 0.375)
    w_coarse = centred(key_of[4], (H, H), H ** -0.5, 0.375)
    w_prolong = centred(key_of[5], (H, H), H ** -0.5, 0.375)
    owner = draw_owner(jax.random.fold_in(key_of[9], 71), 0)
    slot = draw_slot(jax.random.fold_in(key_of[9], 71), 0)
    recv_row = place_ends(jax.random.randint(key_of[8], (SLOTS,), 0, N1_DEV), jax.random.fold_in(key_of[8], 1), 0, N1_DEV - 1).astype(jnp.int32)
    return {"node_feat": node_feat, "coarse_feat": coarse_feat, "cotangent": cotangent, "w_restrict": w_restrict, "w_coarse": w_coarse, "w_prolong": w_prolong, "owner": owner, "slot": slot, "recv_row": recv_row}


def dsilu(value):
    sig = jax.nn.sigmoid(value)
    return sig * (1.0 + value * (1.0 - sig))


def region_pass(feat, coarse, cot, owner, slot, recv_row, w_restrict, w_coarse, w_prolong):
    rows = feat.shape[0]
    device = (jnp.arange(rows, dtype=jnp.int32) // N0_DEV).astype(jnp.int32)
    index = owner * (N_DEV * CAP) + device * CAP + slot
    parent = (owner * N1_DEV + recv_row[index]).astype(jnp.int32)
    count = N_DEV * N1_DEV
    pre = jnp.dot(feat, w_restrict, preferred_element_type=jnp.float32)
    message = jax.nn.silu(pre).astype(jnp.bfloat16)
    summed = coarse.astype(jnp.float32) + jax.ops.segment_sum(message.astype(jnp.float32), parent, num_segments=count)
    summed_b = summed.astype(jnp.bfloat16)
    update = jnp.dot(summed_b, w_coarse, preferred_element_type=jnp.float32)
    coarse_out = (summed + jax.nn.silu(update)).astype(jnp.bfloat16)
    parent_val = coarse_out[parent]
    proj = jnp.dot(parent_val, w_prolong, preferred_element_type=jnp.float32)
    grad_proj = (cot.astype(jnp.float32) * dsilu(proj)).astype(jnp.bfloat16)
    part_wp = jnp.dot(parent_val.T, grad_proj, preferred_element_type=jnp.float32)
    term = jnp.dot(grad_proj, w_prolong.T, preferred_element_type=jnp.float32).astype(jnp.bfloat16)
    grad_out = jax.ops.segment_sum(term.astype(jnp.float32), parent, num_segments=count)
    grad_update = (grad_out * dsilu(update)).astype(jnp.bfloat16)
    grad_summed = grad_out + jnp.dot(grad_update, w_coarse.T, preferred_element_type=jnp.float32)
    grad_coarse = grad_summed.astype(jnp.bfloat16)
    part_wc = jnp.dot(summed_b.T, grad_update, preferred_element_type=jnp.float32)
    grad_pre = (grad_coarse[parent].astype(jnp.float32) * dsilu(pre)).astype(jnp.bfloat16)
    part_wr = jnp.dot(feat.T, grad_pre, preferred_element_type=jnp.float32)
    grad_node = (cot.astype(jnp.float32) + jnp.dot(grad_pre, w_restrict.T, preferred_element_type=jnp.float32)).astype(jnp.bfloat16)
    return grad_node, grad_coarse, part_wr, part_wc, part_wp


def reference(node_feat, coarse_feat, cotangent, w_restrict, w_coarse, w_prolong, owner, slot, recv_row):
    width = node_feat.shape[1]
    feats = node_feat.reshape(N_GRP, N_DEV * N0_DEV, width)
    coarses = coarse_feat.reshape(N_GRP, N_DEV * N1_DEV, width)
    cots = cotangent.reshape(N_GRP, N_DEV * N0_DEV, width)
    owners = owner.reshape(N_GRP, N_DEV * N0_DEV)
    slots = slot.reshape(N_GRP, N_DEV * N0_DEV)
    rows = recv_row.reshape(N_GRP, N_DEV * N_DEV * CAP)

    def run(items):
        return region_pass(items[0], items[1], items[2], items[3], items[4], items[5], w_restrict, w_coarse, w_prolong)

    grad_node, grad_coarse, part_wr, part_wc, part_wp = lax.map(run, (feats, coarses, cots, owners, slots, rows))
    scale = float(N0_DEV * N_DEV * N_GRP) ** -0.5
    return (grad_node.reshape(-1, width), grad_coarse.reshape(-1, width),
            jnp.sum(part_wr, axis=0) * scale, jnp.sum(part_wc, axis=0) * scale, jnp.sum(part_wp, axis=0) * scale)
```

```python
import functools

import jax
import jax.numpy as jnp
from jax import lax
from jax.experimental import pallas as pl
from jax.experimental.pallas import tpu as pltpu
from jax.sharding import PartitionSpec as P

ZN, XN = 8, 4
MESH = pl.DeviceIdType.MESH
SUM_OFFS = (4, 3, -3, 2, -2, 1, -1, 0)
CAST_OFFS = (0, 1, -1, 2, -2, 3, -3, 4)
SUM_AT = {off: t for t, off in enumerate(SUM_OFFS)}
CAST_AT = {off: t for t, off in enumerate(CAST_OFFS)}


def dsilu(value):
    sig = jax.nn.sigmoid(value)
    return sig * (1.0 + value * (1.0 - sig))


def dot(left, right):
    return jnp.dot(left, right, preferred_element_type=jnp.float32)


def right_dot(left, right):
    return lax.dot_general(
        left, right, (((1,), (1,)), ((), ())), preferred_element_type=jnp.float32
    )


def left_dot(left, right):
    return lax.dot_general(
        left, right, (((0,), (0,)), ((), ())), preferred_element_type=jnp.float32
    )


def rows_hot(keys, first, count):
    at = lax.broadcasted_iota(jnp.int32, (count, keys.shape[1]), 0)
    return jnp.where(at == keys - first, 1.0, 0.0).astype(jnp.bfloat16)


def columns_hot(keys, first, count):
    lanes = keys.shape[1]
    at = lax.broadcasted_iota(jnp.int32, keys.shape, 1)
    parts = [
        jnp.where(at == keys - (first + lane), 1.0, 0.0).astype(jnp.bfloat16)
        for lane in range(0, count, lanes)
    ]
    return jnp.concatenate(parts, axis=1)


def turned(keys):
    return jnp.transpose(jnp.broadcast_to(keys, (128, keys.shape[1])))


def coords():
    dev = lax.axis_index("dev")
    return lax.div(dev, XN), lax.rem(dev, XN)


def dev_at(z, x):
    return lax.rem(z + ZN, ZN) * XN + lax.rem(x + XN, XN)


def greet(devices):
    barrier = pltpu.get_barrier_semaphore()
    for device in devices:
        pl.semaphore_signal(barrier, inc=1, device_id=device, device_id_type=MESH)
    pl.semaphore_wait(barrier, len(devices))


def ring_neighbours(z, x):
    return [{"dev": dev_at(z + dz, x + dx)} for dz, dx in ((1, 0), (-1, 0), (0, 1), (0, -1))]


class Rows:
    def __init__(self, z, x, out, into, pass_r, pass_l, send_sem, recv_sem):
        self.refs = (out, into, pass_r, pass_l)
        self.sems = (send_sem, recv_sem)
        self.z, self.x = z, x

    def copies(self, t):
        out, into, pass_r, pass_l = self.refs
        z, x = self.z, self.x
        block = out.shape[1] // XN
        half = block // 2
        right, left, far = lax.rem(x + 1, XN), lax.rem(x + 3, XN), lax.rem(x + 2, XN)

        def part(ref, at, first, count):
            return ref.at[t, pl.ds(pl.multiple_of(at * block + first, half), count)]

        def copy(i, src, dst, to):
            return pltpu.make_async_remote_copy(
                src_ref=src,
                dst_ref=dst,
                send_sem=self.sems[0].at[i, t],
                recv_sem=self.sems[1].at[i, t],
                device_id={"dev": z * XN + to},
                device_id_type=MESH,
            )

        return (
            lambda: copy(0, part(out, far, 0, half), pass_r.at[t], right),
            lambda: copy(1, part(out, far, half, half), pass_l.at[t], left),
            lambda: copy(2, part(out, right, 0, block), part(into, x, 0, block), right),
            lambda: copy(3, part(out, left, 0, block), part(into, x, 0, block), left),
            lambda: copy(4, pass_r.at[t], part(into, left, 0, half), right),
            lambda: copy(5, pass_l.at[t], part(into, right, half, half), left),
        )

    def start(self, t):
        out, into = self.refs[:2]
        block = out.shape[1] // XN
        own = pl.ds(pl.multiple_of(self.x * block, block), block)
        for copy in self.copies(t)[:4]:
            copy().start()
        into[t, own, :] = out[t, own, :]

    def pass_on(self, t):
        copies = self.copies(t)
        for at in (0, 1):
            copies[at]().wait_recv()
            copies[at + 4]().start()

    def arrived(self, t):
        for copy in self.copies(t)[2:]:
            copy().wait_recv()

    def close(self):
        for t in range(ZN):
            for copy in self.copies(t):
                copy().wait_send()


def sum_to_owners(z, x, rows, produce, keys_of, finish, into, out_z, from_lo, from_hi, z_send, z_recv):
    half = out_z.shape[1] // 2

    def hops(off):
        t = SUM_AT[off]
        if off == 4:
            low, high = pl.ds(0, half), pl.ds(half, half)
            return [
                (out_z.at[t, low], from_lo.at[3, low], 0, 3, 1),
                (out_z.at[t, high], from_hi.at[3, high], 1, 3, -1),
            ]
        if off > 0:
            return [(out_z.at[t], from_lo.at[off - 1], 0, off - 1, 1)]
        if off < 0:
            return [(out_z.at[t], from_hi.at[-off - 1], 1, -off - 1, -1)]
        return []

    def z_copies(off):
        def copy(src, dst, side, k, to):
            return pltpu.make_async_remote_copy(
                src_ref=src,
                dst_ref=dst,
                send_sem=z_send.at[side, SUM_AT[off]],
                recv_sem=z_recv.at[side, k],
                device_id={"dev": dev_at(z + to, x)},
                device_id_type=MESH,
            )

        return [functools.partial(copy, *hop) for hop in hops(off)]

    def gather_up(t):
        off = SUM_OFFS[t]
        rows.arrived(t)
        landed = {}
        if 0 <= off < 4:
            (z_copies(4)[0] if off == 3 else z_copies(off + 1)[0])().wait_recv()
            landed[0] = (from_lo, off)
        if -4 < off <= 0:
            (z_copies(4)[1] if off == -3 else z_copies(off - 1)[0])().wait_recv()
            landed[1] = (from_hi, -off)
        keys = keys_of(off)
        for part in range(2):
            span = pl.ds(part * half, half)
            total = dot(rows_hot(keys, part * half, half), into[t])
            for side, (ref, k) in landed.items():
                if k < 3 or side == part:
                    total = total + ref[k, span, :].astype(jnp.float32)
            if off == 0:
                finish(span, total)
            else:
                out_z[t, span, :] = total.astype(jnp.bfloat16)
        for copy in z_copies(off):
            copy().start()

    for t in range(ZN):
        produce(t)
        rows.start(t)
        if t >= 1:
            rows.pass_on(t - 1)
        if t >= 2:
            gather_up(t - 2)
    rows.pass_on(ZN - 1)
    gather_up(ZN - 2)
    gather_up(ZN - 1)
    rows.close()
    for off in SUM_OFFS:
        for copy in z_copies(off):
            copy().wait_send()


def cast_to_children(z, x, rows, keys_of, prepare, consume, out, chunks, z_send, z_recv):
    half = chunks.shape[1] // 2

    def z_copy(src, dst_at, sem_at, to, span=None):
        return functools.partial(z_start, src, dst_at, sem_at, to, span)

    def z_start(src, dst_at, sem_at, to, span):
        src_ref = chunks.at[src] if span is None else chunks.at[src, span]
        dst_ref = chunks.at[dst_at] if span is None else chunks.at[dst_at, span]
        return pltpu.make_async_remote_copy(
            src_ref=src_ref,
            dst_ref=dst_ref,
            send_sem=z_send.at[sem_at],
            recv_sem=z_recv.at[sem_at],
            device_id={"dev": dev_at(z + to, x)},
            device_id_type=MESH,
        )

    low, high = pl.ds(0, half), pl.ds(half, half)

    def z_copies(off):
        t = CAST_AT[off]
        if off == 0:
            return [z_copy(t, CAST_AT[-1], CAST_AT[-1], 1), z_copy(t, CAST_AT[1], CAST_AT[1], -1)]
        if off in (1, 2):
            return [z_copy(t, CAST_AT[off + 1], CAST_AT[off + 1], -1)]
        if off in (-1, -2):
            return [z_copy(t, CAST_AT[off - 1], CAST_AT[off - 1], 1)]
        if off == 3:
            return [z_copy(t, CAST_AT[4], CAST_AT[4], -1, high)]
        if off == -3:
            return [z_copy(t, CAST_AT[4], ZN, 1, low)]
        return []

    def hold(off):
        if off == 0:
            return
        if off == 4:
            z_copies(3)[0]().wait_recv()
            z_copies(-3)[0]().wait_recv()
        elif off == -1:
            z_copies(0)[0]().wait_recv()
        elif off == 1:
            z_copies(0)[1]().wait_recv()
        else:
            z_copies(off - 1 if off > 0 else off + 1)[0]().wait_recv()

    for t in range(ZN):
        off = CAST_OFFS[t]
        hold(off)
        for copy in z_copies(off):
            copy().start()
        keys = keys_of(off)
        count = keys.shape[1] // 2
        for part in range(2):
            span = pl.ds(part * count, count)
            hot = columns_hot(turned(keys[:, part * count:(part + 1) * count]), 0, chunks.shape[1])
            out[t, span, :] = dot(hot, chunks[t]).astype(jnp.bfloat16)
        rows.start(t)
        if t >= 1:
            rows.pass_on(t - 1)
        prepare(t)
        if t >= 2:
            rows.arrived(t - 2)
            consume(t - 2)
    rows.pass_on(ZN - 1)
    for t in (ZN - 2, ZN - 1):
        rows.arrived(t)
        consume(t)
    rows.close()
    for off in CAST_OFFS:
        for copy in z_copies(off):
            copy().wait_send()


def plane(z, off):
    return lax.rem(z + off + ZN, ZN)


def to_slots(slots, values, first, count):
    nodes = values.shape[0]
    step = min(1024, nodes)
    total = jnp.zeros((count, values.shape[1]), jnp.float32)
    for at in range(0, nodes, step):
        total = total + dot(rows_hot(slots[:, at:at + step], first, count), values[at:at + step, :])
    return total.astype(jnp.bfloat16)


def restrict_kernel(
    feat, slots, recv_row, coarse, wr, wc,
    feat_slot, keys_out, summed_b, update, coarse_out,
    keys, out, into, pass_r, pass_l, out_z, from_lo, from_hi,
    send_sem, recv_sem, z_send, z_recv, k_send, k_recv,
):
    z, x = coords()
    greet(
        [{"dev": dev_at(z + dz, x)} for dz in range(1, ZN)]
        + [{"dev": dev_at(z, x + dx)} for dx in (1, -1)]
    )
    key_copies = []
    for dz in range(1, ZN):
        to = plane(z, dz)
        copy = pltpu.make_async_remote_copy(
            src_ref=recv_row.at[to],
            dst_ref=keys.at[z],
            send_sem=k_send.at[dz],
            recv_sem=k_recv.at[dz],
            device_id={"dev": to * XN + x},
            device_id_type=MESH,
        )
        copy.start()
        key_copies.append(copy)
    keys[z] = recv_row[z]
    width = feat_slot.shape[1]
    count = width // 2

    def produce(t):
        first = plane(z, SUM_OFFS[t]) * width

        @pl.loop(0, 2)
        def _(part):
            at = pl.multiple_of(part * count, count)
            block = to_slots(slots, feat, first + at, count)
            feat_slot[t, pl.ds(at, count), :] = block
            pre = dot(block, wr[...])
            out[t, pl.ds(at, count), :] = (pre * jax.nn.sigmoid(pre)).astype(jnp.bfloat16)

        if t == 1:
            for copy in key_copies:
                copy.wait_recv()
            keys_out[...] = keys[...]

    def finish(span, total):
        summed = coarse[span, :].astype(jnp.float32) + total
        rounded = summed.astype(jnp.bfloat16)
        moved = dot(rounded, wc[...])
        summed_b[span, :] = rounded
        update[span, :] = moved
        coarse_out[span, :] = (summed + moved * jax.nn.sigmoid(moved)).astype(jnp.bfloat16)

    rows = Rows(z, x, out, into, pass_r, pass_l, send_sem, recv_sem)
    sum_to_owners(
        z, x, rows, produce, lambda off: keys[plane(z, off)], finish,
        into, out_z, from_lo, from_hi, z_send, z_recv,
    )
    for copy in key_copies:
        copy.wait_send()


def prolong_kernel(
    coarse_out, keys, slots, cot, wp,
    term, part_wp,
    cot_slot, out, into, pass_r, pass_l, chunks,
    send_sem, recv_sem, z_send, z_recv,
):
    z, x = coords()
    greet(ring_neighbours(z, x))
    chunks[0] = coarse_out[...]
    part_wp[...] = jnp.zeros_like(part_wp)
    width = term.shape[1]
    count = width // 2

    def prepare(t):
        first = plane(z, CAST_OFFS[t]) * width

        @pl.loop(0, 2)
        def _(part):
            at = pl.multiple_of(part * count, count)
            cot_slot[t, pl.ds(at, count), :] = to_slots(slots, cot, first + at, count)

    def consume(t):
        @pl.loop(0, 2)
        def _(part):
            span = pl.ds(pl.multiple_of(part * count, count), count)
            parent = into[t, span, :]
            proj = dot(parent, wp[...])
            grad = (cot_slot[t, span, :].astype(jnp.float32) * dsilu(proj)).astype(jnp.bfloat16)
            part_wp[...] += left_dot(parent, grad)
            term[SUM_AT[CAST_OFFS[t]], span, :] = right_dot(grad, wp[...]).astype(jnp.bfloat16)

    rows = Rows(z, x, out, into, pass_r, pass_l, send_sem, recv_sem)
    cast_to_children(
        z, x, rows, lambda off: keys[plane(z, off)], prepare, consume, out, chunks, z_send, z_recv
    )


def coarse_kernel(
    term, keys, summed_b, update, wc,
    grad_coarse, part_wc,
    into, pass_r, pass_l, out_z, from_lo, from_hi,
    send_sem, recv_sem, z_send, z_recv,
):
    z, x = coords()
    greet(ring_neighbours(z, x))
    part_wc[...] = jnp.zeros_like(part_wc)

    def finish(span, total):
        grad_update = (total * dsilu(update[span, :])).astype(jnp.bfloat16)
        grad_coarse[span, :] = (total + right_dot(grad_update, wc[...])).astype(jnp.bfloat16)
        part_wc[...] += left_dot(summed_b[span, :], grad_update)

    rows = Rows(z, x, term, into, pass_r, pass_l, send_sem, recv_sem)
    sum_to_owners(
        z, x, rows, lambda t: None, lambda off: keys[plane(z, off)], finish,
        into, out_z, from_lo, from_hi, z_send, z_recv,
    )


def node_kernel(
    grad_coarse, keys, slots, feat_slot, cot, wr,
    grad_node, part_wr,
    places, grad_pre, back, out, into, pass_r, pass_l, chunks,
    send_sem, recv_sem, z_send, z_recv,
):
    z, x = coords()
    greet(ring_neighbours(z, x))
    chunks[0] = grad_coarse[...]
    part_wr[...] = jnp.zeros_like(part_wr)
    nodes = cot.shape[0]
    width = feat_slot.shape[1]
    count = width // 2
    step = min(512, nodes)

    def prepare(t):
        if t == 0:
            back[...] = jnp.zeros_like(back)
            for at in range(0, nodes, step):
                places[at:at + step, :] = turned(slots[:, at:at + step])

    def consume(t):
        off = CAST_OFFS[t]

        @pl.loop(0, 2)
        def _(part):
            span = pl.ds(pl.multiple_of(part * count, count), count)
            feat = feat_slot[SUM_AT[off], span, :]
            pre = dot(feat, wr[...])
            grad = (into[t, span, :].astype(jnp.float32) * dsilu(pre)).astype(jnp.bfloat16)
            part_wr[...] += left_dot(feat, grad)
            grad_pre[span, :] = grad

        first = plane(z, off) * width

        @pl.loop(0, nodes // step)
        def _(part):
            span = pl.ds(pl.multiple_of(part * step, step), step)
            found = dot(columns_hot(places[span, :], first, width), grad_pre[...])
            back[span, :] = (back[span, :].astype(jnp.float32) + found).astype(jnp.bfloat16)

    rows = Rows(z, x, out, into, pass_r, pass_l, send_sem, recv_sem)
    cast_to_children(
        z, x, rows, lambda off: keys[plane(z, off)], prepare, consume, out, chunks, z_send, z_recv
    )

    @pl.loop(0, nodes // step)
    def _(part):
        span = pl.ds(pl.multiple_of(part * step, step), step)
        grad_node[span, :] = (
            cot[span, :].astype(jnp.float32) + right_dot(back[span, :], wr[...])
        ).astype(jnp.bfloat16)


def total_kernel(scale, parts, totals, by_grp, by_dev, one, row, sems):
    groups, devs = parts.shape[:2]
    g, d = lax.axis_index("grp"), lax.axis_index("dev")

    def other_g(i):
        return lax.rem(g + i, groups)

    def other_d(i):
        return lax.rem(d + i, devs)

    barrier = pltpu.get_barrier_semaphore()

    @pl.loop(1, groups)
    def _(i):
        pl.semaphore_signal(barrier, inc=1, device_id={"grp": other_g(i)}, device_id_type=MESH)

    @pl.loop(1, devs)
    def _(i):
        pl.semaphore_signal(barrier, inc=1, device_id={"dev": other_d(i)}, device_id_type=MESH)

    pl.semaphore_wait(barrier, groups + devs - 2)

    def copy(stage, i, src, dst, to):
        return pltpu.make_async_remote_copy(
            src_ref=src,
            dst_ref=dst,
            send_sem=sems.at[0, stage, i],
            recv_sem=sems.at[1, stage, i],
            device_id=to,
            device_id_type=MESH,
        )

    def run(count, make):
        @pl.loop(1, count)
        def _(i):
            make(i).start()

        @pl.loop(1, count)
        def _(i):
            make(i).wait()

    run(groups, lambda i: copy(0, i, parts.at[other_g(i)], by_grp.at[g], {"grp": other_g(i)}))
    by_grp[g] = parts[g]
    row[...] = jnp.sum(by_grp[...], axis=0)
    run(devs, lambda i: copy(1, i, row.at[other_d(i)], by_dev.at[d], {"dev": other_d(i)}))
    by_dev[d] = row[d]
    one[...] = jnp.sum(by_dev[...], axis=0) * scale
    gathered, spread = totals
    run(devs, lambda i: copy(2, i, one, gathered.at[d], {"dev": other_d(i)}))
    gathered[d] = one[...]
    run(groups, lambda i: copy(3, i, gathered, spread.at[g], {"grp": other_g(i)}))
    spread[g] = gathered[...]


def total_entry(scale, parts, result, by_grp, by_dev, one, row, gathered, spread, sems):
    total_kernel(scale, parts, (gathered, spread), by_grp, by_dev, one, row, sems)
    result[...] = spread[...]


VMEM = pl.BlockSpec(memory_space=pltpu.VMEM)


def call(kernel, args, outs, scratch, collective, limit=60):
    return pl.pallas_call(
        kernel,
        out_shape=outs,
        in_specs=[VMEM] * len(args),
        out_specs=jax.tree.map(lambda _: VMEM, outs),
        scratch_shapes=scratch,
        compiler_params=pltpu.CompilerParams(
            collective_id=collective, has_side_effects=True, vmem_limit_bytes=limit * 2**20
        ),
    )(*args)


def local(
    node_feat, coarse_feat, cotangent, w_restrict, w_coarse, w_prolong, owner, slot, recv_row
):
    devs = ZN * XN
    nodes, width = node_feat.shape
    coarse_rows = coarse_feat.shape[0]
    block = recv_row.shape[0] // devs
    plane_rows = XN * block
    bf, f32 = jnp.bfloat16, jnp.float32
    shape = jax.ShapeDtypeStruct
    dma = pltpu.SemaphoreType.DMA
    slots = (owner * block + slot).reshape(1, nodes)
    keyed = recv_row.reshape(ZN, 1, plane_rows)

    wide = pltpu.VMEM((ZN, plane_rows, width), bf)
    passing = [pltpu.VMEM((ZN, block // 2, width), bf)] * 2
    x_sems = [dma((6, ZN))] * 2
    sum_z = [
        pltpu.VMEM((ZN, coarse_rows, width), bf),
        pltpu.VMEM((4, coarse_rows, width), bf),
        pltpu.VMEM((4, coarse_rows, width), bf),
    ]
    sum_sems = x_sems + [dma((2, ZN)), dma((2, 4))]
    cast_z = [pltpu.VMEM((ZN, coarse_rows, width), bf)]
    cast_sems = x_sems + [dma((ZN + 1,))] * 2

    feat_slot, keys, summed_b, update, coarse_out = call(
        restrict_kernel,
        (node_feat, slots, keyed, coarse_feat, w_restrict, w_coarse),
        (
            shape((ZN, plane_rows, width), bf),
            shape((ZN, 1, plane_rows), jnp.int32),
            shape((coarse_rows, width), bf),
            shape((coarse_rows, width), f32),
            shape((coarse_rows, width), bf),
        ),
        [pltpu.VMEM((ZN, 1, plane_rows), jnp.int32), wide, wide] + passing + sum_z + sum_sems
        + [dma((ZN,))] * 2,
        1,
    )
    term, part_wp = call(
        prolong_kernel,
        (coarse_out, keys, slots, cotangent, w_prolong),
        (shape((ZN, plane_rows, width), bf), shape((width, width), f32)),
        [wide, wide, wide] + passing + cast_z + cast_sems,
        2,
    )
    grad_coarse, part_wc = call(
        coarse_kernel,
        (term, keys, summed_b, update, w_coarse),
        (shape((coarse_rows, width), bf), shape((width, width), f32)),
        [wide] + passing + sum_z + sum_sems,
        3,
    )
    grad_node, part_wr = call(
        node_kernel,
        (grad_coarse, keys, slots, feat_slot, cotangent, w_restrict),
        (shape((nodes, width), bf), shape((width, width), f32)),
        [
            pltpu.VMEM((nodes, 128), jnp.int32),
            pltpu.VMEM((plane_rows, width), bf),
            pltpu.VMEM((nodes, width), bf),
            wide, wide,
        ] + passing + cast_z + cast_sems,
        4,
    )
    groups = lax.axis_size("grp")
    scale = float(nodes * devs * groups) ** (-0.5)
    parts = jnp.stack([part_wr, part_wc, part_wp]).reshape(groups, devs, -1, 128)
    full = parts.shape
    totals = call(
        functools.partial(total_entry, scale),
        (parts,),
        shape(full, f32),
        [
            pltpu.VMEM((groups, devs) + full[2:], f32),
            pltpu.VMEM((devs,) + full[2:], f32),
            pltpu.VMEM(full[2:], f32),
            pltpu.VMEM((devs,) + full[2:], f32),
            pltpu.VMEM((devs,) + full[2:], f32),
            pltpu.VMEM(full, f32),
            dma((2, 4, devs)),
        ],
        5,
    ).reshape(3, width, width)
    return grad_node, grad_coarse, totals[0], totals[1], totals[2]


def solution(mesh):
    return jax.shard_map(
        local,
        mesh=mesh,
        in_specs=(
            P(("grp", "dev"), None),
            P(("grp", "dev"), None),
            P(("grp", "dev"), None),
            P(),
            P(),
            P(),
            P(("grp", "dev")),
            P(("grp", "dev")),
            P(("grp", "dev")),
        ),
        out_specs=(P(("grp", "dev"), None), P(("grp", "dev"), None), P(), P(), P()),
        check_vma=False,
    )
```

```python
import functools

import jax
import jax.numpy as jnp
from jax import lax
from jax.experimental import pallas as pl
from jax.experimental.pallas import tpu as pltpu
from jax.sharding import PartitionSpec as P

ZN, XN = 8, 4
MESH = pl.DeviceIdType.MESH


def dsilu(value):
    sig = jax.nn.sigmoid(value)
    return sig * (1.0 + value * (1.0 - sig))


def dot(left, right):
    return jnp.dot(left, right, preferred_element_type=jnp.float32)


def right_dot(left, right):
    return lax.dot_general(
        left, right, (((1,), (1,)), ((), ())), preferred_element_type=jnp.float32
    )


def left_dot(left, right):
    return lax.dot_general(
        left, right, (((0,), (0,)), ((), ())), preferred_element_type=jnp.float32
    )


def hot(same):
    one = jnp.ones(same.shape, jnp.bfloat16)
    return jnp.where(same, one, jnp.zeros_like(one))


def rows_hot(keys, first, count):
    shape = (count, keys.shape[1])
    at = lax.broadcasted_iota(jnp.int32, shape, 0).astype(jnp.int16)
    return hot(at == jnp.broadcast_to((keys - first).astype(jnp.int16), shape))


def columns_hot(keys, count):
    lanes = keys.shape[1]
    at = lax.broadcasted_iota(jnp.int32, keys.shape, 1)
    parts = [hot((at + lane).astype(jnp.int16) == keys) for lane in range(0, count, lanes)]
    return jnp.concatenate(parts, axis=1)


def turned(keys):
    return jnp.transpose(jnp.broadcast_to(keys, (128, keys.shape[1])))


def sum_off(t):
    return lax.div(8 - t, 2) * (2 * lax.rem(t, 2) - 1)


def cast_off(t):
    return lax.div(t + 1, 2) * (2 * lax.rem(t, 2) - 1)


def remote(src, dst, send_sem, recv_sem, to):
    return pltpu.make_async_remote_copy(
        src_ref=src,
        dst_ref=dst,
        send_sem=send_sem,
        recv_sem=recv_sem,
        device_id=to,
        device_id_type=MESH,
    )


class Here:
    def __init__(self):
        dev = lax.axis_index("dev")
        self.g = lax.axis_index("grp")
        self.z, self.x = lax.div(dev, XN), lax.rem(dev, XN)

    def plane(self, off):
        return lax.rem(self.z + off + ZN, ZN)

    def at_z(self, off):
        return {"dev": self.plane(off) * XN + self.x}

    def at_x(self, x):
        return {"dev": self.z * XN + x}

    def greet(self, groups):
        barrier = pltpu.get_barrier_semaphore()
        partners = [self.at_z(i) for i in range(1, ZN)]
        partners += [self.at_x(lax.rem(self.x + i, XN)) for i in range(1, XN)]
        partners += [{"grp": lax.rem(self.g + i, groups)} for i in range(1, groups)]
        for partner in partners:
            pl.semaphore_signal(barrier, inc=1, device_id=partner, device_id_type=MESH)
        pl.semaphore_wait(barrier, len(partners))


class Rows:
    def __init__(self, here, out, into, pass_r, pass_l, send_sem, recv_sem):
        self.here = here
        self.out, self.into = out, into
        self.passing = pass_r, pass_l
        self.sems = send_sem, recv_sem
        self.block = out.shape[1] // XN

    def copy(self, i, u):
        x, block = self.here.x, self.block
        half = block // 2
        right, left, far = lax.rem(x + 1, XN), lax.rem(x + 3, XN), lax.rem(x + 2, XN)

        def part(ref, at, first, count):
            return ref.at[u, pl.ds(pl.multiple_of(at * block + first, half), count)]

        pass_r, pass_l = self.passing
        if i == 0:
            src, dst, to = part(self.out, far, 0, half), pass_r.at[u], right
        elif i == 1:
            src, dst, to = part(self.out, far, half, half), pass_l.at[u], left
        elif i == 2:
            src, dst, to = part(self.out, right, 0, block), part(self.into, x, 0, block), right
        elif i == 3:
            src, dst, to = part(self.out, left, 0, block), part(self.into, x, 0, block), left
        elif i == 4:
            src, dst, to = pass_r.at[u], part(self.into, left, 0, half), right
        else:
            src, dst, to = pass_l.at[u], part(self.into, right, half, half), left
        return remote(src, dst, self.sems[0].at[i, u], self.sems[1].at[i, u], self.here.at_x(to))

    def start(self, u):
        own = pl.ds(pl.multiple_of(self.here.x * self.block, self.block), self.block)
        for i in range(4):
            self.copy(i, u).start()
        self.into[u, own, :] = self.out[u, own, :]

    def pass_on(self, u):
        for i in (0, 1):
            self.copy(i, u).wait_recv()
            self.copy(i + 4, u).start()

    def arrived(self, u):
        for i in range(2, 6):
            self.copy(i, u).wait_recv()

    def close(self):
        @pl.loop(0, ZN)
        def _(u):
            for i in range(6):
                self.copy(i, u).wait_send()


def sum_to_owners(here, rows, produce, keys, finish, out_z, got, z_send, z_recv):
    half = out_z.shape[1] // 2
    low, high = pl.ds(0, half), pl.ds(half, half)

    def z_copy(t):
        return remote(
            out_z.at[t], got.at[t + 2], z_send.at[t], z_recv.at[t + 2], here.at_z(2 * lax.rem(t, 2) - 1)
        )

    def first_up():
        return remote(out_z.at[0, low], got.at[1, low], z_send.at[0], z_recv.at[1], here.at_z(1))

    def first_down():
        return remote(out_z.at[0, high], got.at[2, high], z_send.at[7], z_recv.at[2], here.at_z(-1))

    def gather_up(t):
        u = here.plane(sum_off(t))
        rows.arrived(u)
        pl.when(t == 1)(lambda: first_up().wait_recv())
        pl.when(t == 2)(lambda: first_down().wait_recv())
        pl.when(t >= 3)(lambda: z_copy(t - 2).wait_recv())
        pl.when(t == ZN - 1)(lambda: z_copy(t - 1).wait_recv())

        @pl.loop(0, 2)
        def _(part):
            first = pl.multiple_of(part * half, half)
            span = pl.ds(first, half)
            total = dot(rows_hot(keys[u], first, half), rows.into[u])
            total = total + got[t, span, :].astype(jnp.float32)

            @pl.when(t == ZN - 1)
            def _():
                finish(span, total + got[ZN, span, :].astype(jnp.float32))

            @pl.when(t < ZN - 1)
            def _():
                out_z[t, span, :] = total.astype(jnp.bfloat16)

        @pl.when(t == 0)
        def _():
            first_up().start()
            first_down().start()

        @pl.when((t > 0) & (t < ZN - 1))
        def _():
            z_copy(t).start()

    @pl.loop(0, ZN + 2)
    def _(i):
        @pl.when(i < ZN)
        def _():
            u = here.plane(sum_off(i))
            produce(i, u)
            rows.start(u)

        @pl.when((i >= 1) & (i <= ZN))
        def _():
            rows.pass_on(here.plane(sum_off(i - 1)))

        @pl.when(i >= 2)
        def _():
            gather_up(i - 2)

    rows.close()
    first_up().wait_send()
    first_down().wait_send()

    @pl.loop(1, ZN - 1)
    def _(t):
        z_copy(t).wait_send()


def cast_to_children(here, rows, keys, prepare, consume, chunks, z_send, z_recv):
    half = chunks.shape[1] // 2
    low, high = pl.ds(0, half), pl.ds(half, half)
    count = rows.out.shape[1] // 2

    def z_copy(t):
        return remote(
            chunks.at[t], chunks.at[t + 2], z_send.at[t], z_recv.at[t + 2], here.at_z(1 - 2 * lax.rem(t, 2))
        )

    def first_down():
        return remote(chunks.at[0], chunks.at[1], z_send.at[0], z_recv.at[1], here.at_z(-1))

    def first_up():
        return remote(chunks.at[0], chunks.at[2], z_send.at[7], z_recv.at[2], here.at_z(1))

    def last_down():
        return remote(chunks.at[5, high], chunks.at[7, high], z_send.at[5], z_recv.at[7], here.at_z(-1))

    def last_up():
        return remote(chunks.at[6, low], chunks.at[7, low], z_send.at[6], z_recv.at[8], here.at_z(1))

    def spread(t, u):
        pl.when(t == 1)(lambda: first_down().wait_recv())
        pl.when(t == 2)(lambda: first_up().wait_recv())
        pl.when((t >= 3) & (t < ZN - 1))(lambda: z_copy(t - 2).wait_recv())

        @pl.when(t == 0)
        def _():
            first_down().start()
            first_up().start()

        pl.when((t > 0) & (t < 5))(lambda: z_copy(t).start())
        pl.when(t == 5)(lambda: last_down().start())
        pl.when(t == 6)(lambda: last_up().start())

        @pl.when(t == ZN - 1)
        def _():
            last_down().wait_recv()
            last_up().wait_recv()

        wanted = keys[u]
        for part in range(2):
            span = pl.ds(part * count, count)
            chosen = columns_hot(
                turned(wanted[:, part * count:(part + 1) * count]).astype(jnp.int16), chunks.shape[1]
            )
            rows.out[u, span, :] = dot(chosen, chunks[t]).astype(jnp.bfloat16)

    @pl.loop(0, ZN + 2)
    def _(i):
        @pl.when(i < ZN)
        def _():
            u = here.plane(cast_off(i))
            spread(i, u)
            rows.start(u)

        @pl.when((i >= 1) & (i <= ZN))
        def _():
            rows.pass_on(here.plane(cast_off(i - 1)))

        prepare(i)

        @pl.when(i >= 2)
        def _():
            u = here.plane(cast_off(i - 2))
            rows.arrived(u)
            consume(i - 2, u)

    rows.close()
    for copy in (first_down, first_up, last_down, last_up):
        copy().wait_send()

    @pl.loop(1, 5)
    def _(t):
        z_copy(t).wait_send()


def to_slots(slots, values, first, count):
    nodes = values.shape[0]
    step = min(1024, nodes)
    total = jnp.zeros((count, values.shape[1]), jnp.float32)
    for at in range(0, nodes, step):
        total = total + dot(rows_hot(slots[:, at:at + step], first, count), values[at:at + step, :])
    return total.astype(jnp.bfloat16)


class Total:
    def __init__(self, here, part, scale, by_g, mid, by_x, one, by_z, done, full_x, full, sems):
        self.here, self.part, self.scale = here, part, scale
        self.by_g, self.mid, self.by_x, self.one = by_g, mid, by_x, one
        self.by_z, self.done, self.full_x, self.full = by_z, done, full_x, full
        self.sems = sems
        self.groups = part.shape[1]

    def peers(self, stage):
        here, groups = self.here, self.groups
        if stage in (0, 4):
            return [lax.rem(here.g + i, groups) for i in range(1, groups)]
        if stage == 2:
            return [here.plane(i) for i in range(1, ZN)]
        return [lax.rem(here.x + i, XN) for i in range(1, XN)]

    def copy(self, stage, i, peer):
        here = self.here
        send, recv = self.sems.at[0, stage, i], self.sems.at[1, stage, i]
        if stage == 0:
            return remote(self.part.at[:, peer], self.by_g.at[:, here.g], send, recv, {"grp": peer})
        if stage == 1:
            return remote(self.mid.at[:, peer], self.by_x.at[:, here.x], send, recv, here.at_x(peer))
        if stage == 2:
            return remote(self.one, self.by_z.at[here.z], send, recv, {"dev": peer * XN + here.x})
        if stage == 3:
            return remote(self.done, self.full_x.at[:, here.x], send, recv, here.at_x(peer))
        return remote(self.full_x, self.full.at[:, here.g], send, recv, {"grp": peer})

    def start(self, stage):
        here = self.here
        for i, peer in enumerate(self.peers(stage)):
            self.copy(stage, i, peer).start()
        if stage == 0:
            self.by_g[:, here.g] = self.part[:, here.g]
        elif stage == 1:
            self.by_x[:, here.x] = self.mid[:, here.x]
        elif stage == 2:
            self.by_z[here.z] = self.one[...]
        elif stage == 3:
            self.full_x[:, here.x] = self.done[...]
        else:
            self.full[:, here.g] = self.full_x[...]

    def end(self, stage):
        for i, peer in enumerate(self.peers(stage)):
            self.copy(stage, i, peer).wait()
        if stage == 0:
            self.mid[...] = jnp.sum(self.by_g[...], axis=1).reshape(self.mid.shape)
        elif stage == 1:
            self.one[...] = jnp.sum(self.by_x[...], axis=1)
        elif stage == 2:
            self.done[...] = jnp.sum(self.by_z[...], axis=0) * self.scale

    def next(self, stage):
        if stage:
            self.end(stage - 1)
        if stage < 5:
            self.start(stage)


def block_kernel(
    scale,
    feat, cot, slots, recv_row, coarse, wr, wc, wp,
    grad_node, grad_coarse, totals,
    keys, feat_slot, cot_slot, out, term,
    summed_b, update, places, grad_pre, back,
    into_a, pass_ra, pass_la, into_b, pass_rb, pass_lb, out_z, got, chunks,
    x_send_a, x_recv_a, x_send_b, x_recv_b, z_send_a, z_recv_a, z_send_b, z_recv_b, k_send, k_recv,
    part_cp, part_r, *total_refs,
):
    here = Here()
    nodes = feat.shape[0]
    width = feat_slot.shape[1]
    count = width // 2
    step = min(512, nodes)
    half = coarse.shape[0] // 2
    groups = part_r.shape[1]
    kept = cot_slot.shape[0]

    got[0] = jnp.zeros_like(got[0])
    got[1, half:, :] = jnp.zeros_like(got[1, half:, :])
    got[2, :half, :] = jnp.zeros_like(got[2, :half, :])
    part_cp[...] = jnp.zeros_like(part_cp)
    part_r[...] = jnp.zeros_like(part_r)
    here.greet(groups)

    def key_copy(off):
        to = here.plane(off)
        return remote(
            recv_row.at[to], keys.at[here.z], k_send.at[off], k_recv.at[off], {"dev": to * XN + here.x}
        )

    for off in range(1, ZN):
        key_copy(off).start()
    keys[here.z] = recv_row[here.z]

    def add(ref, at, value):
        ref[at] += value.reshape(ref.shape[1:])

    def make_message(t, u):
        @pl.loop(0, 2)
        def _(part):
            span = pl.ds(pl.multiple_of(part * count, count), count)
            block = to_slots(slots, feat, u * width + part * count, count)
            feat_slot[u, span, :] = block
            pre = dot(block, wr[...])
            out[u, span, :] = (pre * jax.nn.sigmoid(pre)).astype(jnp.bfloat16)

        @pl.when(t == 1)
        def _():
            for off in range(1, ZN):
                key_copy(off).wait_recv()

    def coarse_update(span, total):
        summed = coarse[span, :].astype(jnp.float32) + total
        rounded = summed.astype(jnp.bfloat16)
        moved = dot(rounded, wc[...])
        summed_b[span, :] = rounded
        update[span, :] = moved
        chunks[0, span, :] = (summed + moved * jax.nn.sigmoid(moved)).astype(jnp.bfloat16)

    rows_a = Rows(here, out, into_a, pass_ra, pass_la, x_send_a, x_recv_a)
    sum_to_owners(here, rows_a, make_message, keys, coarse_update, out_z, got, z_send_a, z_recv_a)
    for off in range(1, ZN):
        key_copy(off).wait_send()

    def place_cotangent(i):
        @pl.when(i < ZN)
        def _():
            first = here.plane(cast_off(i)) * width
            spot = lax.rem(i, kept)

            @pl.loop(0, 2)
            def _(part):
                span = pl.ds(pl.multiple_of(part * count, count), count)
                cot_slot[spot, span, :] = to_slots(slots, cot, first + part * count, count)

    def make_term(t, u):
        spot = lax.rem(t, kept)

        @pl.loop(0, 2)
        def _(part):
            span = pl.ds(pl.multiple_of(part * count, count), count)
            parent = into_b[u, span, :]
            proj = dot(parent, wp[...])
            grad = (cot_slot[spot, span, :].astype(jnp.float32) * dsilu(proj)).astype(jnp.bfloat16)
            add(part_cp, 1, left_dot(parent, grad))
            term[u, span, :] = right_dot(grad, wp[...]).astype(jnp.bfloat16)

    rows_b = Rows(here, out, into_b, pass_rb, pass_lb, x_send_b, x_recv_b)
    cast_to_children(here, rows_b, keys, place_cotangent, make_term, chunks, z_send_b, z_recv_b)

    def coarse_gradient(span, total):
        grad_update = (total * dsilu(update[span, :])).astype(jnp.bfloat16)
        grad = (total + right_dot(grad_update, wc[...])).astype(jnp.bfloat16)
        grad_coarse[span, :] = grad
        chunks[0, span, :] = grad
        add(part_cp, 0, left_dot(summed_b[span, :], grad_update))

    rows_a = Rows(here, term, into_a, pass_ra, pass_la, x_send_a, x_recv_a)
    sum_to_owners(
        here, rows_a, lambda t, u: None, keys, coarse_gradient, out_z, got, z_send_a, z_recv_a
    )

    sums_cp = Total(here, part_cp, scale, *total_refs[:8], total_refs[16])
    sums_r = Total(here, part_r, scale, *total_refs[8:16], total_refs[17])

    def other_sums(i):
        for stage in range(6):
            pl.when(i == stage)(functools.partial(sums_cp.next, stage))

        @pl.when(i == 0)
        def _():
            back[...] = jnp.zeros_like(back)
            for at in range(0, nodes, step):
                places[at:at + step, :] = turned(slots[:, at:at + step])

    def node_gradient(t, u):
        @pl.loop(0, 2)
        def _(part):
            span = pl.ds(pl.multiple_of(part * count, count), count)
            block = feat_slot[u, span, :]
            pre = dot(block, wr[...])
            grad = (into_b[u, span, :].astype(jnp.float32) * dsilu(pre)).astype(jnp.bfloat16)
            add(part_r, 0, left_dot(block, grad))
            grad_pre[span, :] = grad

        pl.when(t == ZN - 1)(functools.partial(sums_r.next, 0))
        first = u * width

        @pl.loop(0, nodes // step)
        def _(part):
            span = pl.ds(pl.multiple_of(part * step, step), step)
            wanted = (places[span, :] - first).astype(jnp.int16)
            found = dot(columns_hot(wanted, width), grad_pre[...])
            back[span, :] = (back[span, :].astype(jnp.float32) + found).astype(jnp.bfloat16)

    rows_b = Rows(here, out, into_b, pass_rb, pass_lb, x_send_b, x_recv_b)
    cast_to_children(here, rows_b, keys, other_sums, node_gradient, chunks, z_send_b, z_recv_b)
    sums_r.next(1)

    @pl.loop(0, nodes // step)
    def _(part):
        span = pl.ds(pl.multiple_of(part * step, step), step)
        grad_node[span, :] = (
            cot[span, :].astype(jnp.float32) + right_dot(back[span, :], wr[...])
        ).astype(jnp.bfloat16)

    for stage in range(2, 6):
        sums_r.next(stage)
    totals[0] = sums_r.full[0].reshape(totals.shape[1:])
    for at in (0, 1):
        totals[at + 1] = sums_cp.full[at].reshape(totals.shape[1:])


def total_scratch(m, groups, width):
    rows = width // groups
    part = rows // XN
    return [
        pltpu.VMEM((m, groups, rows, width), jnp.float32),
        pltpu.VMEM((m, XN, part, width), jnp.float32),
        pltpu.VMEM((m, XN, part, width), jnp.float32),
        pltpu.VMEM((m, part, width), jnp.float32),
        pltpu.VMEM((ZN, m, part, width), jnp.float32),
        pltpu.VMEM((m, part, width), jnp.float32),
        pltpu.VMEM((m, XN, part, width), jnp.float32),
        pltpu.VMEM((m, groups, XN, part, width), jnp.float32),
    ]


def local(
    node_feat, coarse_feat, cotangent, w_restrict, w_coarse, w_prolong, owner, slot, recv_row
):
    devs = ZN * XN
    groups = lax.axis_size("grp")
    nodes, width = node_feat.shape
    coarse_rows = coarse_feat.shape[0]
    block = recv_row.shape[0] // devs
    plane_rows = XN * block
    bf, f32 = jnp.bfloat16, jnp.float32
    shape = jax.ShapeDtypeStruct
    dma = pltpu.SemaphoreType.DMA
    vmem = pltpu.VMEM
    wide = vmem((ZN, plane_rows, width), bf)
    passing = vmem((ZN, block // 2, width), bf)
    scratch = [
        vmem((ZN, 1, plane_rows), jnp.int32),
        wide,
        vmem((4, plane_rows, width), bf),
        wide,
        wide,
        vmem((coarse_rows, width), bf),
        vmem((coarse_rows, width), f32),
        vmem((nodes, 128), jnp.int32),
        vmem((plane_rows, width), bf),
        vmem((nodes, width), bf),
        wide, passing, passing,
        wide, passing, passing,
        vmem((ZN, coarse_rows, width), bf),
        vmem((ZN + 1, coarse_rows, width), bf),
        vmem((ZN, coarse_rows, width), bf),
    ]
    scratch += [dma((6, ZN))] * 4 + [dma((ZN,)), dma((ZN + 1,))] * 2 + [dma((ZN,))] * 2
    scratch += [
        vmem((2, groups, width // groups, width), f32),
        vmem((1, groups, width // groups, width), f32),
    ]
    scratch += total_scratch(2, groups, width) + total_scratch(1, groups, width)
    scratch += [dma((2, 5, ZN))] * 2
    in_vmem = pl.BlockSpec(memory_space=pltpu.VMEM)
    scale = float(nodes * devs * groups) ** (-0.5)
    grad_node, grad_coarse, totals = pl.pallas_call(
        functools.partial(block_kernel, scale),
        out_shape=(
            shape((nodes, width), bf),
            shape((coarse_rows, width), bf),
            shape((3, width, width), f32),
        ),
        in_specs=[in_vmem] * 8,
        out_specs=(in_vmem,) * 3,
        scratch_shapes=scratch,
        compiler_params=pltpu.CompilerParams(
            collective_id=0, has_side_effects=True, vmem_limit_bytes=62 * 2**20
        ),
    )(
        node_feat, cotangent, (owner * block + slot).reshape(1, nodes),
        recv_row.reshape(ZN, 1, plane_rows), coarse_feat, w_restrict, w_coarse, w_prolong,
    )
    return grad_node, grad_coarse, totals[0], totals[1], totals[2]


def solution(mesh):
    return jax.shard_map(
        local,
        mesh=mesh,
        in_specs=(
            P(("grp", "dev"), None),
            P(("grp", "dev"), None),
            P(("grp", "dev"), None),
            P(),
            P(),
            P(),
            P(("grp", "dev")),
            P(("grp", "dev")),
            P(("grp", "dev")),
        ),
        out_specs=(P(("grp", "dev"), None), P(("grp", "dev"), None), P(), P(), P()),
        check_vma=False,
    )
```

```python
import functools

import jax
import jax.numpy as jnp
from jax import lax
from jax.experimental import pallas as pl
from jax.experimental.pallas import tpu as pltpu
from jax.sharding import PartitionSpec as P

ZN, XN = 8, 4
MESH = pl.DeviceIdType.MESH


def dsilu(value):
    sig = jax.nn.sigmoid(value)
    return sig * (1.0 + value * (1.0 - sig))


def dot(left, right):
    return jnp.dot(left, right, preferred_element_type=jnp.float32)


def right_dot(left, right):
    return lax.dot_general(
        left, right, (((1,), (1,)), ((), ())), preferred_element_type=jnp.float32
    )


def left_dot(left, right):
    return lax.dot_general(
        left, right, (((0,), (0,)), ((), ())), preferred_element_type=jnp.float32
    )


def hot(same):
    one = jnp.ones(same.shape, jnp.bfloat16)
    return jnp.where(same, one, jnp.zeros_like(one))


def rows_hot(keys, first, count):
    shape = (count, keys.shape[1])
    at = lax.broadcasted_iota(jnp.int32, shape, 0).astype(jnp.int16)
    return hot(at == jnp.broadcast_to((keys - first).astype(jnp.int16), shape))


def columns_hot(keys, count):
    lanes = keys.shape[1]
    at = lax.broadcasted_iota(jnp.int32, keys.shape, 1)
    parts = [hot((at + lane).astype(jnp.int16) == keys) for lane in range(0, count, lanes)]
    return jnp.concatenate(parts, axis=1)


def turned(keys):
    return jnp.transpose(jnp.broadcast_to(keys, (128, keys.shape[1])))


def sum_off(t):
    return lax.div(8 - t, 2) * (2 * lax.rem(t, 2) - 1)


def cast_off(t):
    return lax.div(t + 1, 2) * (2 * lax.rem(t, 2) - 1)


def remote(src, dst, send_sem, recv_sem, to):
    return pltpu.make_async_remote_copy(
        src_ref=src,
        dst_ref=dst,
        send_sem=send_sem,
        recv_sem=recv_sem,
        device_id=to,
        device_id_type=MESH,
    )


class Here:
    def __init__(self):
        dev = lax.axis_index("dev")
        self.g = lax.axis_index("grp")
        self.z, self.x = lax.div(dev, XN), lax.rem(dev, XN)
        self.right, self.far, self.left = (lax.rem(self.x + i, XN) for i in (1, 2, 3))

    def plane(self, off):
        return lax.rem(self.z + off + ZN, ZN)

    def at_z(self, off):
        return {"dev": self.plane(off) * XN + self.x}

    def at_x(self, x):
        return {"dev": self.z * XN + x}

    def greet(self, groups):
        barrier = pltpu.get_barrier_semaphore()
        partners = [self.at_z(i) for i in range(1, ZN)]
        partners += [{"dev": self.plane(i) * XN + self.far} for i in range(ZN)]
        partners += [self.at_x(self.right), self.at_x(self.left)]
        partners += [{"grp": lax.rem(self.g + i, groups)} for i in range(1, groups)]
        for partner in partners:
            pl.semaphore_signal(barrier, inc=1, device_id=partner, device_id_type=MESH)
        pl.semaphore_wait(barrier, len(partners))


def block_at(x, block):
    return pl.ds(pl.multiple_of(x * block, block), block)


class Rows:
    def __init__(self, here, out, into, send_sem, recv_sem):
        self.here = here
        self.out, self.into = out, into
        self.sems = send_sem, recv_sem
        self.block = out.shape[1] // XN

    def copy(self, i, u):
        to = self.here.left if i else self.here.right
        return remote(
            self.out.at[u, block_at(to, self.block)],
            self.into.at[u, block_at(self.here.x, self.block)],
            self.sems[0].at[i, u],
            self.sems[1].at[i, u],
            self.here.at_x(to),
        )

    def start(self, u):
        own = block_at(self.here.x, self.block)
        for i in (0, 1):
            self.copy(i, u).start()
        self.into[u, own, :] = self.out[u, own, :]

    def arrived(self, u):
        for i in (0, 1):
            self.copy(i, u).wait_recv()

    def close(self):
        @pl.loop(0, ZN)
        def _(u):
            for i in (0, 1):
                self.copy(i, u).wait_send()


class Across:
    def __init__(self, here, src, dst, pass_r, pass_l, send_sem, recv_sem):
        self.here, self.src, self.dst = here, src, dst
        self.passing = pass_r, pass_l
        self.sems = send_sem, recv_sem
        self.half = src.shape[0] // 2

    def copy(self, i):
        span = pl.ds(i % 2 * self.half, self.half)
        buffer = self.passing[i % 2]
        src, dst = (self.src.at[span], buffer) if i < 2 else (buffer, self.dst.at[span])
        to = self.here.at_x(self.here.left if i % 2 else self.here.right)
        return remote(src, dst, self.sems[0].at[i], self.sems[1].at[i], to)

    def start(self):
        for i in (0, 1):
            self.copy(i).start()

    def pass_on(self):
        for i in (0, 1):
            self.copy(i).wait_recv()
            self.copy(i + 2).start()

    def arrived(self):
        for i in (2, 3):
            self.copy(i).wait_recv()

    def close(self):
        for i in range(4):
            self.copy(i).wait_send()


class SumChain:
    def __init__(self, here, out, got, send_sem, recv_sem):
        self.here, self.out, self.got = here, out, got
        self.send, self.recv = send_sem, recv_sem
        half = out.shape[1] // 2
        self.low, self.high = pl.ds(0, half), pl.ds(half, half)

    def copy(self, t):
        to = self.here.at_z(2 * lax.rem(t, 2) - 1)
        return remote(self.out.at[t], self.got.at[t + 2], self.send.at[t], self.recv.at[t + 2], to)

    def first_up(self):
        src, dst = self.out.at[0, self.low], self.got.at[1, self.low]
        return remote(src, dst, self.send.at[0], self.recv.at[1], self.here.at_z(1))

    def first_down(self):
        src, dst = self.out.at[0, self.high], self.got.at[2, self.high]
        return remote(src, dst, self.send.at[7], self.recv.at[2], self.here.at_z(-1))

    def clear(self):
        for at in (self.got.at[0], self.got.at[1, self.high], self.got.at[2, self.low]):
            at[...] = jnp.zeros(at.shape, at.dtype)

    def hold(self, t):
        pl.when(t == 1)(lambda: self.first_up().wait_recv())
        pl.when(t == 2)(lambda: self.first_down().wait_recv())
        pl.when(t >= 3)(lambda: self.copy(t - 2).wait_recv())
        pl.when(t == ZN - 1)(lambda: self.copy(t - 1).wait_recv())

    def start(self, t):
        @pl.when(t == 0)
        def _():
            self.first_up().start()
            self.first_down().start()

        pl.when((t > 0) & (t < ZN - 1))(lambda: self.copy(t).start())

    def close(self):
        self.first_up().wait_send()
        self.first_down().wait_send()

        @pl.loop(1, ZN - 1)
        def _(t):
            self.copy(t).wait_send()


class CastChain:
    def __init__(self, here, chunks, send_sem, recv_sem):
        self.here, self.chunks = here, chunks
        self.send, self.recv = send_sem, recv_sem
        half = chunks.shape[1] // 2
        self.low, self.high = pl.ds(0, half), pl.ds(half, half)

    def copy(self, t):
        to = self.here.at_z(1 - 2 * lax.rem(t, 2))
        return remote(self.chunks.at[t], self.chunks.at[t + 2], self.send.at[t], self.recv.at[t + 2], to)

    def first_down(self):
        src, dst = self.chunks.at[0], self.chunks.at[1]
        return remote(src, dst, self.send.at[0], self.recv.at[1], self.here.at_z(-1))

    def first_up(self):
        src, dst = self.chunks.at[0], self.chunks.at[2]
        return remote(src, dst, self.send.at[7], self.recv.at[2], self.here.at_z(1))

    def last_down(self):
        src, dst = self.chunks.at[5, self.high], self.chunks.at[7, self.high]
        return remote(src, dst, self.send.at[5], self.recv.at[7], self.here.at_z(-1))

    def last_up(self):
        src, dst = self.chunks.at[6, self.low], self.chunks.at[7, self.low]
        return remote(src, dst, self.send.at[6], self.recv.at[8], self.here.at_z(1))

    def step(self, t):
        pl.when(t == 1)(lambda: self.first_down().wait_recv())
        pl.when(t == 2)(lambda: self.first_up().wait_recv())
        pl.when((t >= 3) & (t < ZN - 1))(lambda: self.copy(t - 2).wait_recv())

        @pl.when(t == 0)
        def _():
            self.first_down().start()
            self.first_up().start()

        pl.when((t > 0) & (t < 5))(lambda: self.copy(t).start())
        pl.when(t == 5)(lambda: self.last_down().start())
        pl.when(t == 6)(lambda: self.last_up().start())

        @pl.when(t == ZN - 1)
        def _():
            self.last_down().wait_recv()
            self.last_up().wait_recv()

    def close(self):
        for copy in (self.first_down, self.first_up, self.last_down, self.last_up):
            copy().wait_send()

        @pl.loop(1, 5)
        def _(t):
            self.copy(t).wait_send()


def sum_to_owners(here, rows, near, far, across, produce, keys, far_keys, finish):
    half = near.out.shape[1] // 2

    def far_up(t, u):
        far.hold(t)
        values = rows.out[u, block_at(here.far, rows.block), :]

        @pl.loop(0, 2)
        def _(part):
            first = pl.multiple_of(part * half, half)
            span = pl.ds(first, half)
            total = dot(rows_hot(far_keys[u], first, half), values)
            total = total + far.got[t, span, :].astype(jnp.float32)

            @pl.when(t == ZN - 1)
            def _():
                last = far.got[ZN, span, :].astype(jnp.float32)
                across.src[span, :] = (total + last).astype(jnp.bfloat16)

            @pl.when(t < ZN - 1)
            def _():
                far.out[t, span, :] = total.astype(jnp.bfloat16)

        far.start(t)
        pl.when(t == ZN - 1)(across.start)

    def near_up(t):
        u = here.plane(sum_off(t))
        rows.arrived(u)
        near.hold(t)
        pl.when(t == ZN - 1)(across.arrived)

        @pl.loop(0, 2)
        def _(part):
            first = pl.multiple_of(part * half, half)
            span = pl.ds(first, half)
            total = dot(rows_hot(keys[u], first, half), rows.into[u])
            total = total + near.got[t, span, :].astype(jnp.float32)

            @pl.when(t == ZN - 1)
            def _():
                last = near.got[ZN, span, :].astype(jnp.float32)
                finish(span, total + last + across.dst[span, :].astype(jnp.float32))

            @pl.when(t < ZN - 1)
            def _():
                near.out[t, span, :] = total.astype(jnp.bfloat16)

        near.start(t)

    @pl.loop(0, ZN + 2)
    def _(i):
        @pl.when(i < ZN)
        def _():
            u = here.plane(sum_off(i))
            produce(i, u)
            rows.start(u)
            far_up(i, u)

        pl.when(i == ZN)(across.pass_on)
        pl.when(i >= 2)(lambda: near_up(i - 2))

    for part in (rows, near, far, across):
        part.close()


def cast_to_children(here, rows, near, far, across, keys, far_keys, prepare, consume):
    def chosen(wanted, chunk):
        places = turned(wanted).astype(jnp.int16)
        return dot(columns_hot(places, chunk.shape[0]), chunk).astype(jnp.bfloat16)

    @pl.loop(0, ZN + 2)
    def _(i):
        @pl.when(i < ZN)
        def _():
            near.step(i)
            pl.when(i == 0)(across.start)
            u = here.plane(cast_off(i))

            @pl.loop(0, 3)
            def _(j):
                span = block_at(lax.rem(here.x + 3 + j, XN), rows.block)
                rows.out[u, span, :] = chosen(keys[u, :, span], near.chunks[i])

            rows.start(u)

        pl.when(i == 1)(across.arrived)
        pl.when((i >= 1) & (i <= ZN))(lambda: far.step(i - 1))
        prepare(i)
        pl.when(i == 0)(across.pass_on)

        @pl.when(i >= 2)
        def _():
            u = here.plane(cast_off(i - 2))
            rows.into[u, block_at(here.far, rows.block), :] = chosen(far_keys[u], far.chunks[i - 2])
            rows.arrived(u)
            consume(i - 2, u)

    for part in (rows, near, far, across):
        part.close()


def to_slots(slots, values, first, count):
    nodes = values.shape[0]
    step = min(1024, nodes)
    total = jnp.zeros((count, values.shape[1]), jnp.float32)
    for at in range(0, nodes, step):
        total = total + dot(rows_hot(slots[:, at:at + step], first, count), values[at:at + step, :])
    return total.astype(jnp.bfloat16)


class Total:
    def __init__(self, here, part, scale, by_g, mid, by_x, one, by_z, done, full_x, full, sems):
        self.here, self.part, self.scale = here, part, scale
        self.by_g, self.mid, self.by_x, self.one = by_g, mid, by_x, one
        self.by_z, self.done, self.full_x, self.full = by_z, done, full_x, full
        self.sems = sems
        self.groups = part.shape[1]

    def peers(self, stage):
        here, groups = self.here, self.groups
        if stage in (0, 4):
            return [lax.rem(here.g + i, groups) for i in range(1, groups)]
        if stage == 2:
            return [here.plane(i) for i in range(1, ZN)]
        return [lax.rem(here.x + i, XN) for i in range(1, XN)]

    def copy(self, stage, i, peer):
        here = self.here
        send, recv = self.sems.at[0, stage, i], self.sems.at[1, stage, i]
        if stage == 0:
            return remote(self.part.at[:, peer], self.by_g.at[:, here.g], send, recv, {"grp": peer})
        if stage == 1:
            return remote(self.mid.at[:, peer], self.by_x.at[:, here.x], send, recv, here.at_x(peer))
        if stage == 2:
            return remote(self.one, self.by_z.at[here.z], send, recv, {"dev": peer * XN + here.x})
        if stage == 3:
            return remote(self.done, self.full_x.at[:, here.x], send, recv, here.at_x(peer))
        return remote(self.full_x, self.full.at[:, here.g], send, recv, {"grp": peer})

    def start(self, stage):
        here = self.here
        for i, peer in enumerate(self.peers(stage)):
            self.copy(stage, i, peer).start()
        if stage == 0:
            self.by_g[:, here.g] = self.part[:, here.g]
        elif stage == 1:
            self.by_x[:, here.x] = self.mid[:, here.x]
        elif stage == 2:
            self.by_z[here.z] = self.one[...]
        elif stage == 3:
            self.full_x[:, here.x] = self.done[...]
        else:
            self.full[:, here.g] = self.full_x[...]

    def end(self, stage):
        for i, peer in enumerate(self.peers(stage)):
            self.copy(stage, i, peer).wait()
        if stage == 0:
            self.mid[...] = jnp.sum(self.by_g[...], axis=1).reshape(self.mid.shape)
        elif stage == 1:
            self.one[...] = jnp.sum(self.by_x[...], axis=1)
        elif stage == 2:
            self.done[...] = jnp.sum(self.by_z[...], axis=0) * self.scale

    def next(self, stage):
        if stage:
            self.end(stage - 1)
        if stage < 5:
            self.start(stage)


def block_kernel(
    scale,
    feat, cot, slots, recv_row, coarse, wr, wc, wp,
    grad_node, grad_coarse, total_r, total_c, total_p,
    keys, far_keys, feat_slot, cot_slot, out, term,
    summed_b, update, places, grad_pre, back,
    into_a, into_b, near_out, near_got, far_out, far_got, near_chunks, far_chunks,
    far_sum, far_in, pass_ra, pass_la, pass_rb, pass_lb,
    x_send_a, x_recv_a, x_send_b, x_recv_b, f_send_a, f_recv_a, f_send_b, f_recv_b,
    zn_send_a, zn_recv_a, zn_send_b, zn_recv_b, zf_send_a, zf_recv_a, zf_send_b, zf_recv_b,
    k_send, k_recv, part_cp, part_r, *total_refs,
):
    here = Here()
    nodes = feat.shape[0]
    width = feat_slot.shape[1]
    count = width // 2
    step = min(512, nodes)
    groups = part_r.shape[1]
    kept = cot_slot.shape[0]
    block = width // XN

    near_sums = SumChain(here, near_out, near_got, zn_send_a, zn_recv_a)
    far_sums = SumChain(here, far_out, far_got, zf_send_a, zf_recv_a)
    far_back = Across(here, far_sum, far_in, pass_ra, pass_la, f_send_a, f_recv_a)
    near_cast = CastChain(here, near_chunks, zn_send_b, zn_recv_b)
    far_cast = CastChain(here, far_chunks, zf_send_b, zf_recv_b)
    far_over = Across(here, near_chunks.at[0], far_chunks.at[0], pass_rb, pass_lb, f_send_b, f_recv_b)
    near_sums.clear()
    far_sums.clear()
    into_a[:, block_at(here.far, block), :] = jnp.zeros((ZN, block, into_a.shape[2]), into_a.dtype)
    part_cp[...] = jnp.zeros_like(part_cp)
    part_r[...] = jnp.zeros_like(part_r)
    here.greet(groups)

    def key_copy(off):
        to = here.plane(off)
        return remote(
            recv_row.at[to], keys.at[here.z], k_send.at[off], k_recv.at[off], {"dev": to * XN + here.x}
        )

    def far_key_copy(off):
        to = here.plane(off)
        return remote(
            recv_row.at[to, :, block_at(here.far, block)],
            far_keys.at[here.z],
            k_send.at[ZN + off],
            k_recv.at[ZN + off],
            {"dev": to * XN + here.far},
        )

    key_copies = [functools.partial(far_key_copy, off) for off in range(ZN)]
    key_copies += [functools.partial(key_copy, off) for off in range(1, ZN)]
    for copy in key_copies:
        copy().start()
    keys[here.z] = recv_row[here.z]

    def add(ref, at, value):
        ref[at] += value.reshape(ref.shape[1:])

    def make_message(t, u):
        @pl.loop(0, 2)
        def _(part):
            span = pl.ds(pl.multiple_of(part * count, count), count)
            found = to_slots(slots, feat, u * width + part * count, count)
            feat_slot[u, span, :] = found
            pre = dot(found, wr[...])
            out[u, span, :] = (pre * jax.nn.sigmoid(pre)).astype(jnp.bfloat16)

        @pl.when(t == 0)
        def _():
            for copy in key_copies:
                copy().wait_recv()

    def coarse_update(span, total):
        summed = coarse[span, :].astype(jnp.float32) + total
        rounded = summed.astype(jnp.bfloat16)
        moved = dot(rounded, wc[...])
        summed_b[span, :] = rounded
        update[span, :] = moved
        near_chunks[0, span, :] = (summed + moved * jax.nn.sigmoid(moved)).astype(jnp.bfloat16)

    rows_a = Rows(here, out, into_a, x_send_a, x_recv_a)
    sum_to_owners(
        here, rows_a, near_sums, far_sums, far_back, make_message, keys, far_keys, coarse_update
    )
    for copy in key_copies:
        copy().wait_send()

    def place_cotangent(i):
        @pl.when(i < ZN)
        def _():
            first = here.plane(cast_off(i)) * width
            spot = lax.rem(i, kept)

            @pl.loop(0, 2)
            def _(part):
                span = pl.ds(pl.multiple_of(part * count, count), count)
                cot_slot[spot, span, :] = to_slots(slots, cot, first + part * count, count)

    def make_term(t, u):
        spot = lax.rem(t, kept)

        @pl.loop(0, 2)
        def _(part):
            span = pl.ds(pl.multiple_of(part * count, count), count)
            parent = into_b[u, span, :]
            proj = dot(parent, wp[...])
            grad = (cot_slot[spot, span, :].astype(jnp.float32) * dsilu(proj)).astype(jnp.bfloat16)
            add(part_cp, 1, left_dot(parent, grad))
            term[u, span, :] = right_dot(grad, wp[...]).astype(jnp.bfloat16)

    rows_b = Rows(here, out, into_b, x_send_b, x_recv_b)
    cast_to_children(
        here, rows_b, near_cast, far_cast, far_over, keys, far_keys, place_cotangent, make_term
    )

    def coarse_gradient(span, total):
        grad_update = (total * dsilu(update[span, :])).astype(jnp.bfloat16)
        grad = (total + right_dot(grad_update, wc[...])).astype(jnp.bfloat16)
        grad_coarse[span, :] = grad
        near_chunks[0, span, :] = grad
        add(part_cp, 0, left_dot(summed_b[span, :], grad_update))

    rows_a = Rows(here, term, into_a, x_send_a, x_recv_a)
    sum_to_owners(
        here, rows_a, near_sums, far_sums, far_back, lambda t, u: None, keys, far_keys, coarse_gradient
    )

    sums_cp = Total(here, part_cp, scale, *total_refs[:8], total_refs[16])
    sums_r = Total(here, part_r, scale, *total_refs[8:16], total_refs[17])

    def other_sums(i):
        for stage in range(6):
            pl.when(i == stage)(functools.partial(sums_cp.next, stage))

        @pl.when(i == 0)
        def _():
            back[...] = jnp.zeros_like(back)
            for at in range(0, nodes, step):
                places[at:at + step, :] = turned(slots[:, at:at + step])

    def node_gradient(t, u):
        @pl.loop(0, 2)
        def _(part):
            span = pl.ds(pl.multiple_of(part * count, count), count)
            found = feat_slot[u, span, :]
            pre = dot(found, wr[...])
            grad = (into_b[u, span, :].astype(jnp.float32) * dsilu(pre)).astype(jnp.bfloat16)
            add(part_r, 0, left_dot(found, grad))
            grad_pre[span, :] = grad

        pl.when(t == ZN - 1)(functools.partial(sums_r.next, 0))
        first = u * width

        @pl.loop(0, nodes // step)
        def _(part):
            span = pl.ds(pl.multiple_of(part * step, step), step)
            wanted = (places[span, :] - first).astype(jnp.int16)
            found = dot(columns_hot(wanted, width), grad_pre[...])
            back[span, :] = (back[span, :].astype(jnp.float32) + found).astype(jnp.bfloat16)

    cast_to_children(
        here, rows_b, near_cast, far_cast, far_over, keys, far_keys, other_sums, node_gradient
    )
    sums_r.next(1)

    @pl.loop(0, nodes // step)
    def _(part):
        span = pl.ds(pl.multiple_of(part * step, step), step)
        grad_node[span, :] = (
            cot[span, :].astype(jnp.float32) + right_dot(back[span, :], wr[...])
        ).astype(jnp.bfloat16)

    for stage in range(2, 6):
        sums_r.next(stage)
    total_r[...] = sums_r.full[0].reshape(total_r.shape)
    total_c[...] = sums_cp.full[0].reshape(total_c.shape)
    total_p[...] = sums_cp.full[1].reshape(total_p.shape)


def total_scratch(m, groups, width):
    rows = width // groups
    part = rows // XN
    return [
        pltpu.VMEM((m, groups, rows, width), jnp.float32),
        pltpu.VMEM((m, XN, part, width), jnp.float32),
        pltpu.VMEM((m, XN, part, width), jnp.float32),
        pltpu.VMEM((m, part, width), jnp.float32),
        pltpu.VMEM((ZN, m, part, width), jnp.float32),
        pltpu.VMEM((m, part, width), jnp.float32),
        pltpu.VMEM((m, XN, part, width), jnp.float32),
        pltpu.VMEM((m, groups, XN, part, width), jnp.float32),
    ]


def local(
    node_feat, coarse_feat, cotangent, w_restrict, w_coarse, w_prolong, owner, slot, recv_row
):
    devs = ZN * XN
    groups = lax.axis_size("grp")
    nodes, width = node_feat.shape
    coarse_rows = coarse_feat.shape[0]
    block = recv_row.shape[0] // devs
    plane_rows = XN * block
    bf, f32 = jnp.bfloat16, jnp.float32
    shape = jax.ShapeDtypeStruct
    dma = pltpu.SemaphoreType.DMA
    vmem = pltpu.VMEM
    wide = vmem((ZN, plane_rows, width), bf)
    chain = vmem((ZN, coarse_rows, width), bf)
    chain_in = vmem((ZN + 1, coarse_rows, width), bf)
    chunk = vmem((coarse_rows, width), bf)
    passing = vmem((coarse_rows // 2, width), bf)
    scratch = [
        vmem((ZN, 1, plane_rows), jnp.int32),
        vmem((ZN, 1, block), jnp.int32),
        wide,
        vmem((4, plane_rows, width), bf),
        wide,
        wide,
        chunk,
        vmem((coarse_rows, width), f32),
        vmem((nodes, 128), jnp.int32),
        vmem((plane_rows, width), bf),
        vmem((nodes, width), bf),
        wide, wide,
        chain, chain_in, chain, chain_in, chain, chain,
        chunk, chunk, passing, passing, passing, passing,
    ]
    scratch += [dma((2, ZN))] * 4 + [dma((4,))] * 4 + [dma((ZN,)), dma((ZN + 1,))] * 4
    scratch += [dma((2 * ZN,))] * 2
    scratch += [
        vmem((2, groups, width // groups, width), f32),
        vmem((1, groups, width // groups, width), f32),
    ]
    scratch += total_scratch(2, groups, width) + total_scratch(1, groups, width)
    scratch += [dma((2, 5, ZN))] * 2
    in_vmem = pl.BlockSpec(memory_space=pltpu.VMEM)
    scale = float(nodes * devs * groups) ** (-0.5)
    weight = shape((width, width), f32)
    return pl.pallas_call(
        functools.partial(block_kernel, scale),
        out_shape=(
            shape((nodes, width), bf),
            shape((coarse_rows, width), bf),
            weight, weight, weight,
        ),
        in_specs=[in_vmem] * 8,
        out_specs=(in_vmem,) * 5,
        scratch_shapes=scratch,
        compiler_params=pltpu.CompilerParams(
            collective_id=0, has_side_effects=True, vmem_limit_bytes=62 * 2**20
        ),
    )(
        node_feat, cotangent, (owner * block + slot).reshape(1, nodes),
        recv_row.reshape(ZN, 1, plane_rows), coarse_feat, w_restrict, w_coarse, w_prolong,
    )

def solution(mesh):
    return jax.shard_map(
        local,
        mesh=mesh,
        in_specs=(
            P(("grp", "dev"), None),
            P(("grp", "dev"), None),
            P(("grp", "dev"), None),
            P(),
            P(),
            P(),
            P(("grp", "dev")),
            P(("grp", "dev")),
            P(("grp", "dev")),
        ),
        out_specs=(P(("grp", "dev"), None), P(("grp", "dev"), None), P(), P(), P()),
        check_vma=False,
    )
```

```python
import functools

import jax
import jax.numpy as jnp
from jax import lax
from jax.experimental import pallas as pl
from jax.experimental.pallas import tpu as pltpu
from jax.sharding import PartitionSpec as P

ZN, XN = 8, 4
MESH = pl.DeviceIdType.MESH


def dsilu(value):
    sig = jax.nn.sigmoid(value)
    return sig * (1.0 + value * (1.0 - sig))


def dot(left, right):
    return jnp.dot(left, right, preferred_element_type=jnp.float32)


def right_dot(left, right):
    return lax.dot_general(
        left, right, (((1,), (1,)), ((), ())), preferred_element_type=jnp.float32
    )


def left_dot(left, right):
    return lax.dot_general(
        left, right, (((0,), (0,)), ((), ())), preferred_element_type=jnp.float32
    )


def hot(same):
    one = jnp.ones(same.shape, jnp.bfloat16)
    return jnp.where(same, one, jnp.zeros_like(one))


def rows_hot(keys, first, count):
    lanes = min(128, keys.shape[1])
    at = lax.broadcasted_iota(jnp.int32, (count, lanes), 0).astype(jnp.int16)
    wanted = (keys - first).astype(jnp.int16)
    parts = [
        hot(at == jnp.broadcast_to(wanted[:, lane:lane + lanes], at.shape))
        for lane in range(0, keys.shape[1], lanes)
    ]
    return jnp.concatenate(parts, axis=1)


def columns_hot(keys, count):
    rows, lanes = keys.shape
    tile = min(16, rows)
    at = lax.broadcasted_iota(jnp.int32, (1, tile, lanes), 2)
    tiled = keys.reshape(rows // tile, tile, lanes)
    parts = [
        hot(tiled == jnp.broadcast_to((at + lane).astype(jnp.int16), tiled.shape)).reshape(rows, lanes)
        for lane in range(0, count, lanes)
    ]
    return jnp.concatenate(parts, axis=1)


def turned(keys):
    return jnp.transpose(jnp.broadcast_to(keys, (128, keys.shape[1])))


def sum_off(t):
    return lax.div(8 - t, 2) * (2 * lax.rem(t, 2) - 1)


def cast_off(t):
    return lax.div(t + 1, 2) * (2 * lax.rem(t, 2) - 1)


def remote(src, dst, send_sem, recv_sem, to):
    return pltpu.make_async_remote_copy(
        src_ref=src,
        dst_ref=dst,
        send_sem=send_sem,
        recv_sem=recv_sem,
        device_id=to,
        device_id_type=MESH,
    )


class Here:
    def __init__(self):
        dev = lax.axis_index("dev")
        self.g = lax.axis_index("grp")
        self.z, self.x = lax.div(dev, XN), lax.rem(dev, XN)

    def plane(self, off):
        return lax.rem(self.z + off + ZN, ZN)

    def at_z(self, off):
        return {"dev": self.plane(off) * XN + self.x}

    def at_x(self, x):
        return {"dev": self.z * XN + x}

    def greet(self, groups):
        barrier = pltpu.get_barrier_semaphore()
        partners = [self.at_z(i) for i in range(1, ZN)]
        partners += [self.at_x(lax.rem(self.x + i, XN)) for i in range(1, XN)]
        partners += [{"grp": lax.rem(self.g + i, groups)} for i in range(1, groups)]
        for partner in partners:
            pl.semaphore_signal(barrier, inc=1, device_id=partner, device_id_type=MESH)
        pl.semaphore_wait(barrier, len(partners))


class Rows:
    def __init__(self, here, out, into, pass_r, pass_l, send_sem, recv_sem):
        self.here = here
        self.out, self.into = out, into
        self.passing = pass_r, pass_l
        self.sems = send_sem, recv_sem
        self.block = out.shape[1] // XN

    def copy(self, i, u):
        x, block = self.here.x, self.block
        half = block // 2
        right, left, far = lax.rem(x + 1, XN), lax.rem(x + 3, XN), lax.rem(x + 2, XN)

        def part(ref, at, first, count):
            return ref.at[u, pl.ds(pl.multiple_of(at * block + first, half), count)]

        pass_r, pass_l = self.passing
        if i == 0:
            src, dst, to = part(self.out, far, 0, half), pass_r.at[u], right
        elif i == 1:
            src, dst, to = part(self.out, far, half, half), pass_l.at[u], left
        elif i == 2:
            src, dst, to = part(self.out, right, 0, block), part(self.into, x, 0, block), right
        elif i == 3:
            src, dst, to = part(self.out, left, 0, block), part(self.into, x, 0, block), left
        elif i == 4:
            src, dst, to = pass_r.at[u], part(self.into, left, 0, half), right
        else:
            src, dst, to = pass_l.at[u], part(self.into, right, half, half), left
        return remote(src, dst, self.sems[0].at[i, u], self.sems[1].at[i, u], self.here.at_x(to))

    def start(self, u):
        own = pl.ds(pl.multiple_of(self.here.x * self.block, self.block), self.block)
        for i in range(4):
            self.copy(i, u).start()
        self.into[u, own, :] = self.out[u, own, :]

    def pass_on(self, u):
        for i in (0, 1):
            self.copy(i, u).wait_recv()
            self.copy(i + 4, u).start()

    def arrived(self, u):
        for i in range(2, 6):
            self.copy(i, u).wait_recv()

    def close(self):
        @pl.loop(0, ZN)
        def _(u):
            for i in range(6):
                self.copy(i, u).wait_send()


def sum_to_owners(here, rows, produce, keys, finish, out_z, got, z_send, z_recv):
    half = out_z.shape[1] // 2
    low, high = pl.ds(0, half), pl.ds(half, half)

    def z_copy(t):
        return remote(
            out_z.at[t], got.at[t + 2], z_send.at[t], z_recv.at[t + 2], here.at_z(2 * lax.rem(t, 2) - 1)
        )

    def first_up():
        return remote(out_z.at[0, low], got.at[1, low], z_send.at[0], z_recv.at[1], here.at_z(1))

    def first_down():
        return remote(out_z.at[0, high], got.at[2, high], z_send.at[7], z_recv.at[2], here.at_z(-1))

    def gather_up(t):
        u = here.plane(sum_off(t))
        rows.arrived(u)
        pl.when(t == 1)(lambda: first_up().wait_recv())
        pl.when(t == 2)(lambda: first_down().wait_recv())
        pl.when(t >= 3)(lambda: z_copy(t - 2).wait_recv())
        pl.when(t == ZN - 1)(lambda: z_copy(t - 1).wait_recv())

        def total(part):
            span = pl.ds(part * half, half)
            found = dot(rows_hot(keys[u], part * half, half), rows.into[u])
            return span, found + got[t, span, :].astype(jnp.float32)

        @pl.when(t == ZN - 1)
        def _():
            for part in range(2):
                span, found = total(part)
                finish(span, found + got[ZN, span, :].astype(jnp.float32))

        @pl.when(t < ZN - 1)
        def _():
            for part in range(2):
                span, found = total(part)
                out_z[t, span, :] = found.astype(jnp.bfloat16)

        @pl.when(t == 0)
        def _():
            first_up().start()
            first_down().start()

        @pl.when((t > 0) & (t < ZN - 1))
        def _():
            z_copy(t).start()

    @pl.loop(0, ZN + 2)
    def _(i):
        @pl.when(i < ZN)
        def _():
            u = here.plane(sum_off(i))
            produce(i, u)
            rows.start(u)

        @pl.when((i >= 1) & (i <= ZN))
        def _():
            rows.pass_on(here.plane(sum_off(i - 1)))

        @pl.when(i >= 2)
        def _():
            gather_up(i - 2)

    rows.close()
    first_up().wait_send()
    first_down().wait_send()

    @pl.loop(1, ZN - 1)
    def _(t):
        z_copy(t).wait_send()


def cast_to_children(here, rows, places_of, prepare, consume, chunks, z_send, z_recv):
    half = chunks.shape[1] // 2
    low, high = pl.ds(0, half), pl.ds(half, half)
    count = rows.out.shape[1] // 2

    def z_copy(t):
        return remote(
            chunks.at[t], chunks.at[t + 2], z_send.at[t], z_recv.at[t + 2], here.at_z(1 - 2 * lax.rem(t, 2))
        )

    def first_down():
        return remote(chunks.at[0], chunks.at[1], z_send.at[0], z_recv.at[1], here.at_z(-1))

    def first_up():
        return remote(chunks.at[0], chunks.at[2], z_send.at[7], z_recv.at[2], here.at_z(1))

    def last_down():
        return remote(chunks.at[5, high], chunks.at[7, high], z_send.at[5], z_recv.at[7], here.at_z(-1))

    def last_up():
        return remote(chunks.at[6, low], chunks.at[7, low], z_send.at[6], z_recv.at[8], here.at_z(1))

    def spread(t, u):
        pl.when(t == 1)(lambda: first_down().wait_recv())
        pl.when(t == 2)(lambda: first_up().wait_recv())
        pl.when((t >= 3) & (t < ZN - 1))(lambda: z_copy(t - 2).wait_recv())

        @pl.when(t == 0)
        def _():
            first_down().start()
            first_up().start()

        pl.when((t > 0) & (t < 5))(lambda: z_copy(t).start())
        pl.when(t == 5)(lambda: last_down().start())
        pl.when(t == 6)(lambda: last_up().start())

        @pl.when(t == ZN - 1)
        def _():
            last_down().wait_recv()
            last_up().wait_recv()

        for part in range(2):
            span = pl.ds(part * count, count)
            chosen = columns_hot(places_of(u, part * count, count), chunks.shape[1])
            rows.out[u, span, :] = dot(chosen, chunks[t]).astype(jnp.bfloat16)

    @pl.loop(0, ZN + 2)
    def _(i):
        @pl.when(i < ZN)
        def _():
            u = here.plane(cast_off(i))
            spread(i, u)
            rows.start(u)

        @pl.when((i >= 1) & (i <= ZN))
        def _():
            rows.pass_on(here.plane(cast_off(i - 1)))

        prepare(i)

        @pl.when(i >= 2)
        def _():
            u = here.plane(cast_off(i - 2))
            rows.arrived(u)
            consume(i - 2, u)

    rows.close()
    for copy in (first_down, first_up, last_down, last_up):
        copy().wait_send()

    @pl.loop(1, 5)
    def _(t):
        z_copy(t).wait_send()


def to_slots(slots, values, first, count):
    nodes = values.shape[0]
    step = min(1024, nodes)
    total = jnp.zeros((count, values.shape[1]), jnp.float32)
    for at in range(0, nodes, step):
        total = total + dot(rows_hot(slots[:, at:at + step], first, count), values[at:at + step, :])
    return total.astype(jnp.bfloat16)


class Total:
    def __init__(self, here, part, scale, by_g, mid, by_x, one, by_z, done, full_x, full, sems):
        self.here, self.part, self.scale = here, part, scale
        self.by_g, self.mid, self.by_x, self.one = by_g, mid, by_x, one
        self.by_z, self.done, self.full_x, self.full = by_z, done, full_x, full
        self.sems = sems
        self.groups = part.shape[1]

    def peers(self, stage):
        here, groups = self.here, self.groups
        if stage in (0, 4):
            return [lax.rem(here.g + i, groups) for i in range(1, groups)]
        if stage == 2:
            return [here.plane(i) for i in range(1, ZN)]
        return [lax.rem(here.x + i, XN) for i in range(1, XN)]

    def copy(self, stage, i, peer):
        here = self.here
        send, recv = self.sems.at[0, stage, i], self.sems.at[1, stage, i]
        if stage == 0:
            return remote(self.part.at[:, peer], self.by_g.at[:, here.g], send, recv, {"grp": peer})
        if stage == 1:
            return remote(self.mid.at[:, peer], self.by_x.at[:, here.x], send, recv, here.at_x(peer))
        if stage == 2:
            return remote(self.one, self.by_z.at[here.z], send, recv, {"dev": peer * XN + here.x})
        if stage == 3:
            return remote(self.done, self.full_x.at[:, here.x], send, recv, here.at_x(peer))
        return remote(self.full_x, self.full.at[:, here.g], send, recv, {"grp": peer})

    def start(self, stage):
        here = self.here
        for i, peer in enumerate(self.peers(stage)):
            self.copy(stage, i, peer).start()
        if stage == 0:
            self.by_g[:, here.g] = self.part[:, here.g]
        elif stage == 1:
            self.by_x[:, here.x] = self.mid[:, here.x]
        elif stage == 2:
            self.by_z[here.z] = self.one[...]
        elif stage == 3:
            self.full_x[:, here.x] = self.done[...]
        else:
            self.full[:, here.g] = self.full_x[...]

    def end(self, stage):
        for i, peer in enumerate(self.peers(stage)):
            self.copy(stage, i, peer).wait()
        if stage == 0:
            self.mid[...] = jnp.sum(self.by_g[...], axis=1).reshape(self.mid.shape)
        elif stage == 1:
            self.one[...] = jnp.sum(self.by_x[...], axis=1)
        elif stage == 2:
            self.done[...] = jnp.sum(self.by_z[...], axis=0) * self.scale

    def next(self, stage):
        if stage:
            self.end(stage - 1)
        if stage < 5:
            self.start(stage)


def block_kernel(
    scale,
    feat, cot, slots, recv_row, coarse, wr, wc, wp,
    grad_node, grad_coarse, total_r, total_c, total_p,
    keys, feat_slot, cot_slot, out, term,
    summed_b, update, key_places, places, grad_pre, back,
    into_a, pass_ra, pass_la, into_b, pass_rb, pass_lb, out_z, got, chunks,
    x_send_a, x_recv_a, x_send_b, x_recv_b, z_send_a, z_recv_a, z_send_b, z_recv_b, k_send, k_recv,
    part_cp, part_r, *total_refs,
):
    here = Here()
    nodes = feat.shape[0]
    width = feat_slot.shape[1]
    count = width // 2
    step = min(512, nodes)
    half = coarse.shape[0] // 2
    groups = part_r.shape[1]

    got[0] = jnp.zeros_like(got[0])
    got[1, half:, :] = jnp.zeros_like(got[1, half:, :])
    got[2, :half, :] = jnp.zeros_like(got[2, :half, :])
    part_cp[...] = jnp.zeros_like(part_cp)
    part_r[...] = jnp.zeros_like(part_r)
    here.greet(groups)

    def key_copy(off):
        to = here.plane(off)
        return remote(
            recv_row.at[to], keys.at[here.z], k_send.at[off], k_recv.at[off], {"dev": to * XN + here.x}
        )

    for off in range(1, ZN):
        key_copy(off).start()
    keys[here.z] = recv_row[here.z]

    def add(ref, at, value):
        ref[at] += value.reshape(ref.shape[1:])

    def make_message(t, u):
        for part in range(2):
            span = pl.ds(part * count, count)
            block = to_slots(slots, feat, u * width + part * count, count)
            feat_slot[u, span, :] = block
            pre = dot(block, wr[...])
            out[u, span, :] = (pre * jax.nn.sigmoid(pre)).astype(jnp.bfloat16)

        @pl.when(t == 1)
        def _():
            for off in range(1, ZN):
                key_copy(off).wait_recv()

    def coarse_update(span, total):
        summed = coarse[span, :].astype(jnp.float32) + total
        rounded = summed.astype(jnp.bfloat16)
        moved = dot(rounded, wc[...])
        summed_b[span, :] = rounded
        update[span, :] = moved
        chunks[0, span, :] = (summed + moved * jax.nn.sigmoid(moved)).astype(jnp.bfloat16)

    rows_a = Rows(here, out, into_a, pass_ra, pass_la, x_send_a, x_recv_a)
    sum_to_owners(here, rows_a, make_message, keys, coarse_update, out_z, got, z_send_a, z_recv_a)
    for off in range(1, ZN):
        key_copy(off).wait_send()

    def place_cotangent(i):
        @pl.when(i < ZN)
        def _():
            u = here.plane(cast_off(i))
            for part in range(2):
                span = pl.ds(part * count, count)
                cot_slot[u, span, :] = to_slots(slots, cot, u * width + part * count, count)

    def new_places(u, first, count):
        found = turned(keys[u, :, first:first + count]).astype(jnp.int16)
        key_places[u, first:first + count, :] = found
        return found

    def old_places(u, first, count):
        return key_places[u, first:first + count, :]

    def make_term(t, u):
        for part in range(2):
            span = pl.ds(part * count, count)
            parent = into_b[u, span, :]
            proj = dot(parent, wp[...])
            grad = (cot_slot[u, span, :].astype(jnp.float32) * dsilu(proj)).astype(jnp.bfloat16)
            add(part_cp, 1, left_dot(parent, grad))
            term[u, span, :] = right_dot(grad, wp[...]).astype(jnp.bfloat16)

        @pl.when(t == 2)
        def _():
            back[...] = jnp.zeros_like(back)
            for at in range(0, nodes, step):
                places[at:at + step, :] = turned(slots[:, at:at + step]).astype(jnp.int16)

    rows_b = Rows(here, out, into_b, pass_rb, pass_lb, x_send_b, x_recv_b)
    cast_to_children(
        here, rows_b, new_places, place_cotangent, lambda t, u: None, chunks, z_send_b, z_recv_b
    )

    def coarse_gradient(span, total):
        grad_update = (total * dsilu(update[span, :])).astype(jnp.bfloat16)
        grad = (total + right_dot(grad_update, wc[...])).astype(jnp.bfloat16)
        grad_coarse[span, :] = grad
        chunks[0, span, :] = grad
        add(part_cp, 0, left_dot(summed_b[span, :], grad_update))

    rows_a = Rows(here, term, into_a, pass_ra, pass_la, x_send_a, x_recv_a)
    sum_to_owners(
        here, rows_a, make_term, keys, coarse_gradient, out_z, got, z_send_a, z_recv_a
    )

    sums_cp = Total(here, part_cp, scale, *total_refs[:8], total_refs[16])
    sums_r = Total(here, part_r, scale, *total_refs[8:16], total_refs[17])

    def other_sums(i):
        for stage in range(6):
            pl.when(i == stage)(functools.partial(sums_cp.next, stage))

    def node_gradient(t, u):
        for part in range(2):
            span = pl.ds(part * count, count)
            block = feat_slot[u, span, :]
            pre = dot(block, wr[...])
            grad = (into_b[u, span, :].astype(jnp.float32) * dsilu(pre)).astype(jnp.bfloat16)
            add(part_r, 0, left_dot(block, grad))
            grad_pre[span, :] = grad

        pl.when(t == ZN - 1)(functools.partial(sums_r.next, 0))
        first = jnp.full((step, places.shape[1]), u * width, jnp.int32).astype(jnp.int16)

        @pl.loop(0, nodes // step, unroll=2)
        def _(part):
            span = pl.ds(pl.multiple_of(part * step, step), step)
            wanted = places[span, :] - first
            found = dot(columns_hot(wanted, width), grad_pre[...])
            back[span, :] = (back[span, :].astype(jnp.float32) + found).astype(jnp.bfloat16)

    rows_b = Rows(here, out, into_b, pass_rb, pass_lb, x_send_b, x_recv_b)
    cast_to_children(here, rows_b, old_places, other_sums, node_gradient, chunks, z_send_b, z_recv_b)
    sums_r.next(1)

    @pl.loop(0, nodes // step)
    def _(part):
        span = pl.ds(pl.multiple_of(part * step, step), step)
        grad_node[span, :] = (
            cot[span, :].astype(jnp.float32) + right_dot(back[span, :], wr[...])
        ).astype(jnp.bfloat16)

    for stage in range(2, 6):
        sums_r.next(stage)
    total_r[...] = sums_r.full[0].reshape(total_r.shape)
    total_c[...] = sums_cp.full[0].reshape(total_c.shape)
    total_p[...] = sums_cp.full[1].reshape(total_p.shape)


def total_scratch(m, groups, width):
    rows = width // groups
    part = rows // XN
    return [
        pltpu.VMEM((m, groups, rows, width), jnp.float32),
        pltpu.VMEM((m, XN, part, width), jnp.float32),
        pltpu.VMEM((m, XN, part, width), jnp.float32),
        pltpu.VMEM((m, part, width), jnp.float32),
        pltpu.VMEM((ZN, m, part, width), jnp.float32),
        pltpu.VMEM((m, part, width), jnp.float32),
        pltpu.VMEM((m, XN, part, width), jnp.float32),
        pltpu.VMEM((m, groups, XN, part, width), jnp.float32),
    ]


def local(
    node_feat, coarse_feat, cotangent, w_restrict, w_coarse, w_prolong, owner, slot, recv_row
):
    devs = ZN * XN
    groups = lax.axis_size("grp")
    nodes, width = node_feat.shape
    coarse_rows = coarse_feat.shape[0]
    block = recv_row.shape[0] // devs
    plane_rows = XN * block
    bf, f32 = jnp.bfloat16, jnp.float32
    shape = jax.ShapeDtypeStruct
    dma = pltpu.SemaphoreType.DMA
    vmem = pltpu.VMEM
    wide = vmem((ZN, plane_rows, width), bf)
    passing = vmem((ZN, block // 2, width), bf)
    scratch = [
        vmem((ZN, 1, plane_rows), jnp.int32),
        wide,
        wide,
        wide,
        wide,
        vmem((coarse_rows, width), bf),
        vmem((coarse_rows, width), f32),
        vmem((ZN, plane_rows, 128), jnp.int16),
        vmem((nodes, 128), jnp.int16),
        vmem((plane_rows, width), bf),
        vmem((nodes, width), bf),
        wide, passing, passing,
        wide, passing, passing,
        vmem((ZN, coarse_rows, width), bf),
        vmem((ZN + 1, coarse_rows, width), bf),
        vmem((ZN, coarse_rows, width), bf),
    ]
    scratch += [dma((6, ZN))] * 4 + [dma((ZN,)), dma((ZN + 1,))] * 2 + [dma((ZN,))] * 2
    scratch += [
        vmem((2, groups, width // groups, width), f32),
        vmem((1, groups, width // groups, width), f32),
    ]
    scratch += total_scratch(2, groups, width) + total_scratch(1, groups, width)
    scratch += [dma((2, 5, ZN))] * 2
    in_vmem = pl.BlockSpec(memory_space=pltpu.VMEM)
    scale = float(nodes * devs * groups) ** (-0.5)
    weight = shape((width, width), f32)
    return pl.pallas_call(
        functools.partial(block_kernel, scale),
        out_shape=(
            shape((nodes, width), bf),
            shape((coarse_rows, width), bf),
            weight, weight, weight,
        ),
        in_specs=[in_vmem] * 8,
        out_specs=(in_vmem,) * 5,
        scratch_shapes=scratch,
        compiler_params=pltpu.CompilerParams(
            collective_id=0, has_side_effects=True, vmem_limit_bytes=62 * 2**20
        ),
    )(
        node_feat, cotangent, (owner * block + slot).reshape(1, nodes),
        recv_row.reshape(ZN, 1, plane_rows), coarse_feat, w_restrict, w_coarse, w_prolong,
    )

def solution(mesh):
    return jax.shard_map(
        local,
        mesh=mesh,
        in_specs=(
            P(("grp", "dev"), None),
            P(("grp", "dev"), None),
            P(("grp", "dev"), None),
            P(),
            P(),
            P(),
            P(("grp", "dev")),
            P(("grp", "dev")),
            P(("grp", "dev")),
        ),
        out_specs=(P(("grp", "dev"), None), P(("grp", "dev"), None), P(), P(), P()),
        check_vma=False,
    )
```

```python
import functools

import jax
import jax.numpy as jnp
from jax import lax
from jax.experimental import pallas as pl
from jax.experimental.pallas import tpu as pltpu
from jax.sharding import PartitionSpec as P

ZN, XN = 8, 4
MESH = pl.DeviceIdType.MESH


def dsilu(value):
    sig = jax.nn.sigmoid(value)
    return sig * (1.0 + value * (1.0 - sig))


def dot(left, right):
    return jnp.dot(left, right, preferred_element_type=jnp.float32)


def right_dot(left, right):
    return lax.dot_general(
        left, right, (((1,), (1,)), ((), ())), preferred_element_type=jnp.float32
    )


def left_dot(left, right):
    return lax.dot_general(
        left, right, (((0,), (0,)), ((), ())), preferred_element_type=jnp.float32
    )


def hot(same):
    one = jnp.ones(same.shape, jnp.bfloat16)
    return jnp.where(same, one, jnp.zeros_like(one))


def rows_hot(keys, first, count):
    lanes = min(128, keys.shape[1])
    at = lax.broadcasted_iota(jnp.int32, (count, lanes), 0).astype(jnp.int16)
    wanted = (keys - first).astype(jnp.int16)
    parts = [
        hot(at == jnp.broadcast_to(wanted[:, lane:lane + lanes], at.shape))
        for lane in range(0, keys.shape[1], lanes)
    ]
    return jnp.concatenate(parts, axis=1)


def columns_hot(keys, count):
    rows, lanes = keys.shape
    tile = min(16, rows)
    at = lax.broadcasted_iota(jnp.int32, (1, tile, lanes), 2)
    tiled = keys.reshape(rows // tile, tile, lanes)
    parts = [
        hot(tiled == jnp.broadcast_to((at + lane).astype(jnp.int16), tiled.shape)).reshape(rows, lanes)
        for lane in range(0, count, lanes)
    ]
    return jnp.concatenate(parts, axis=1)


def turned(keys):
    return jnp.transpose(jnp.broadcast_to(keys, (128, keys.shape[1])))


def sum_off(t):
    return lax.div(8 - t, 2) * (2 * lax.rem(t, 2) - 1)


def cast_off(t):
    return lax.div(t + 1, 2) * (2 * lax.rem(t, 2) - 1)


def remote(src, dst, send_sem, recv_sem, to):
    return pltpu.make_async_remote_copy(
        src_ref=src,
        dst_ref=dst,
        send_sem=send_sem,
        recv_sem=recv_sem,
        device_id=to,
        device_id_type=MESH,
    )


class Here:
    def __init__(self):
        dev = lax.axis_index("dev")
        self.g = lax.axis_index("grp")
        self.z, self.x = lax.div(dev, XN), lax.rem(dev, XN)

    def plane(self, off):
        return lax.rem(self.z + off + ZN, ZN)

    def at_z(self, off):
        return {"dev": self.plane(off) * XN + self.x}

    def at_x(self, x):
        return {"dev": self.z * XN + x}

    def greet(self, groups):
        barrier = pltpu.get_barrier_semaphore()
        partners = [self.at_z(i) for i in range(1, ZN)]
        partners += [self.at_x(lax.rem(self.x + i, XN)) for i in range(1, XN)]
        partners += [{"grp": lax.rem(self.g + i, groups)} for i in range(1, groups)]
        for partner in partners:
            pl.semaphore_signal(barrier, inc=1, device_id=partner, device_id_type=MESH)
        pl.semaphore_wait(barrier, len(partners))


class Rows:
    def __init__(self, here, out, into, pass_r, pass_l, send_sem, recv_sem):
        self.here = here
        self.out, self.into = out, into
        self.passing = pass_r, pass_l
        self.sems = send_sem, recv_sem
        self.block = out.shape[1] // XN

    def copy(self, i, u):
        x, block = self.here.x, self.block
        half = block // 2
        right, left, far = lax.rem(x + 1, XN), lax.rem(x + 3, XN), lax.rem(x + 2, XN)

        def part(ref, at, first, count):
            return ref.at[u, pl.ds(pl.multiple_of(at * block + first, half), count)]

        pass_r, pass_l = self.passing
        if i == 0:
            src, dst, to = part(self.out, far, 0, half), pass_r.at[u], right
        elif i == 1:
            src, dst, to = part(self.out, far, half, half), pass_l.at[u], left
        elif i == 2:
            src, dst, to = part(self.out, right, 0, block), part(self.into, x, 0, block), right
        elif i == 3:
            src, dst, to = part(self.out, left, 0, block), part(self.into, x, 0, block), left
        elif i == 4:
            src, dst, to = pass_r.at[u], part(self.into, left, 0, half), right
        else:
            src, dst, to = pass_l.at[u], part(self.into, right, half, half), left
        return remote(src, dst, self.sems[0].at[i, u], self.sems[1].at[i, u], self.here.at_x(to))

    def start(self, u):
        own = pl.ds(pl.multiple_of(self.here.x * self.block, self.block), self.block)
        for i in range(4):
            self.copy(i, u).start()
        self.into[u, own, :] = self.out[u, own, :]

    def pass_on(self, u):
        for i in (0, 1):
            self.copy(i, u).wait_recv()
            self.copy(i + 4, u).start()

    def arrived(self, u):
        for i in range(2, 6):
            self.copy(i, u).wait_recv()

    def close(self):
        @pl.loop(0, ZN)
        def _(u):
            for i in range(6):
                self.copy(i, u).wait_send()


def sum_to_owners(here, rows, produce, keys, finish, out_z, got, z_send, z_recv):
    half = out_z.shape[1] // 2
    low, high = pl.ds(0, half), pl.ds(half, half)

    def z_copy(t):
        return remote(
            out_z.at[t], got.at[t + 2], z_send.at[t], z_recv.at[t + 2], here.at_z(2 * lax.rem(t, 2) - 1)
        )

    def first_up():
        return remote(out_z.at[0, low], got.at[1, low], z_send.at[0], z_recv.at[1], here.at_z(1))

    def first_down():
        return remote(out_z.at[0, high], got.at[2, high], z_send.at[7], z_recv.at[2], here.at_z(-1))

    def gather_up(t):
        u = here.plane(sum_off(t))
        rows.arrived(u)
        pl.when(t == 1)(lambda: first_up().wait_recv())
        pl.when(t == 2)(lambda: first_down().wait_recv())
        pl.when(t >= 3)(lambda: z_copy(t - 2).wait_recv())
        pl.when(t == ZN - 1)(lambda: z_copy(t - 1).wait_recv())

        def total(part):
            span = pl.ds(part * half, half)
            found = dot(rows_hot(keys[u], part * half, half), rows.into[u])
            return span, found + got[t, span, :].astype(jnp.float32)

        @pl.when(t == ZN - 1)
        def _():
            for part in range(2):
                span, found = total(part)
                finish(span, found + got[ZN, span, :].astype(jnp.float32))

        @pl.when(t < ZN - 1)
        def _():
            for part in range(2):
                span, found = total(part)
                out_z[t, span, :] = found.astype(jnp.bfloat16)

        @pl.when(t == 0)
        def _():
            first_up().start()
            first_down().start()

        @pl.when((t > 0) & (t < ZN - 1))
        def _():
            z_copy(t).start()

    @pl.loop(0, ZN + 2)
    def _(i):
        @pl.when(i < ZN)
        def _():
            u = here.plane(sum_off(i))
            produce(i, u)

        @pl.when((i >= 1) & (i <= ZN))
        def _():
            rows.pass_on(here.plane(sum_off(i - 1)))

        @pl.when(i < ZN)
        def _():
            rows.start(here.plane(sum_off(i)))

        @pl.when(i >= 2)
        def _():
            gather_up(i - 2)

    rows.close()
    first_up().wait_send()
    first_down().wait_send()

    @pl.loop(1, ZN - 1)
    def _(t):
        z_copy(t).wait_send()


def cast_to_children(here, rows, places_of, prepare, consume, chunks, z_send, z_recv):
    half = chunks.shape[1] // 2
    low, high = pl.ds(0, half), pl.ds(half, half)
    count = rows.out.shape[1] // 2

    def z_copy(t):
        return remote(
            chunks.at[t], chunks.at[t + 2], z_send.at[t], z_recv.at[t + 2], here.at_z(1 - 2 * lax.rem(t, 2))
        )

    def first_down():
        return remote(chunks.at[0], chunks.at[1], z_send.at[0], z_recv.at[1], here.at_z(-1))

    def first_up():
        return remote(chunks.at[0], chunks.at[2], z_send.at[7], z_recv.at[2], here.at_z(1))

    def last_down():
        return remote(chunks.at[5, high], chunks.at[7, high], z_send.at[5], z_recv.at[7], here.at_z(-1))

    def last_up():
        return remote(chunks.at[6, low], chunks.at[7, low], z_send.at[6], z_recv.at[8], here.at_z(1))

    def spread(t, u):
        pl.when(t == 1)(lambda: first_down().wait_recv())
        pl.when(t == 2)(lambda: first_up().wait_recv())
        pl.when((t >= 3) & (t < ZN - 1))(lambda: z_copy(t - 2).wait_recv())

        @pl.when(t == 0)
        def _():
            first_down().start()
            first_up().start()

        pl.when((t > 0) & (t < 5))(lambda: z_copy(t).start())
        pl.when(t == 5)(lambda: last_down().start())
        pl.when(t == 6)(lambda: last_up().start())

        @pl.when(t == ZN - 1)
        def _():
            last_down().wait_recv()
            last_up().wait_recv()

        for part in range(2):
            span = pl.ds(part * count, count)
            chosen = columns_hot(places_of(u, part * count, count), chunks.shape[1])
            rows.out[u, span, :] = dot(chosen, chunks[t]).astype(jnp.bfloat16)

    @pl.loop(0, ZN + 2)
    def _(i):
        @pl.when(i < ZN)
        def _():
            u = here.plane(cast_off(i))
            spread(i, u)

        @pl.when((i >= 1) & (i <= ZN))
        def _():
            rows.pass_on(here.plane(cast_off(i - 1)))

        @pl.when(i < ZN)
        def _():
            rows.start(here.plane(cast_off(i)))

        prepare(i)

        @pl.when(i >= 2)
        def _():
            u = here.plane(cast_off(i - 2))
            rows.arrived(u)
            consume(i - 2, u)

    rows.close()
    for copy in (first_down, first_up, last_down, last_up):
        copy().wait_send()

    @pl.loop(1, 5)
    def _(t):
        z_copy(t).wait_send()


def to_slots(slots, values, first, count):
    nodes = values.shape[0]
    step = min(1024, nodes)
    total = jnp.zeros((count, values.shape[1]), jnp.float32)
    for at in range(0, nodes, step):
        total = total + dot(rows_hot(slots[:, at:at + step], first, count), values[at:at + step, :])
    return total.astype(jnp.bfloat16)


class Total:
    def __init__(self, here, part, scale, by_g, mid, by_x, one, by_z, done, full_x, full, sems):
        self.here, self.part, self.scale = here, part, scale
        self.by_g, self.mid, self.by_x, self.one = by_g, mid, by_x, one
        self.by_z, self.done, self.full_x, self.full = by_z, done, full_x, full
        self.sems = sems
        self.groups = part.shape[1]

    def peers(self, stage):
        here, groups = self.here, self.groups
        if stage in (0, 4):
            return [lax.rem(here.g + i, groups) for i in range(1, groups)]
        if stage == 2:
            return [here.plane(i) for i in range(1, ZN)]
        return [lax.rem(here.x + i, XN) for i in range(1, XN)]

    def copy(self, stage, i, peer):
        here = self.here
        send, recv = self.sems.at[0, stage, i], self.sems.at[1, stage, i]
        if stage == 0:
            return remote(self.part.at[:, peer], self.by_g.at[:, here.g], send, recv, {"grp": peer})
        if stage == 1:
            return remote(self.mid.at[:, peer], self.by_x.at[:, here.x], send, recv, here.at_x(peer))
        if stage == 2:
            return remote(self.one, self.by_z.at[here.z], send, recv, {"dev": peer * XN + here.x})
        if stage == 3:
            return remote(self.done, self.full_x.at[:, here.x], send, recv, here.at_x(peer))
        return remote(self.full_x, self.full.at[:, here.g], send, recv, {"grp": peer})

    def start(self, stage):
        here = self.here
        for i, peer in enumerate(self.peers(stage)):
            self.copy(stage, i, peer).start()
        if stage == 0:
            self.by_g[:, here.g] = self.part[:, here.g]
        elif stage == 1:
            self.by_x[:, here.x] = self.mid[:, here.x]
        elif stage == 2:
            self.by_z[here.z] = self.one[...]
        elif stage == 3:
            self.full_x[:, here.x] = self.done[...]
        else:
            self.full[:, here.g] = self.full_x[...]

    def end(self, stage):
        for i, peer in enumerate(self.peers(stage)):
            self.copy(stage, i, peer).wait()
        if stage == 0:
            self.mid[...] = jnp.sum(self.by_g[...], axis=1).reshape(self.mid.shape)
        elif stage == 1:
            self.one[...] = jnp.sum(self.by_x[...], axis=1)
        elif stage == 2:
            self.done[...] = jnp.sum(self.by_z[...], axis=0) * self.scale

    def next(self, stage):
        if stage:
            self.end(stage - 1)
        if stage < 5:
            self.start(stage)


def block_kernel(
    scale,
    feat, cot, slots, recv_row, coarse, wr, wc, wp,
    grad_node, grad_coarse, total_r, total_c, total_p,
    keys, feat_slot, cot_slot, out, term,
    summed_b, update, key_places, places, grad_pre, back,
    into_a, pass_ra, pass_la, into_b, pass_rb, pass_lb, out_z, got, chunks,
    x_send_a, x_recv_a, x_send_b, x_recv_b, z_send_a, z_recv_a, z_send_b, z_recv_b, k_send, k_recv,
    part_cp, part_r, *total_refs,
):
    here = Here()
    nodes = feat.shape[0]
    width = feat_slot.shape[1]
    count = width // 2
    step = min(512, nodes)
    half = coarse.shape[0] // 2
    groups = part_r.shape[1]

    got[0] = jnp.zeros_like(got[0])
    got[1, half:, :] = jnp.zeros_like(got[1, half:, :])
    got[2, :half, :] = jnp.zeros_like(got[2, :half, :])
    part_cp[...] = jnp.zeros_like(part_cp)
    part_r[...] = jnp.zeros_like(part_r)
    here.greet(groups)

    def key_copy(off):
        to = here.plane(off)
        return remote(
            recv_row.at[to], keys.at[here.z], k_send.at[off], k_recv.at[off], {"dev": to * XN + here.x}
        )

    for off in range(1, ZN):
        key_copy(off).start()
    keys[here.z] = recv_row[here.z]

    def add(ref, at, value):
        ref[at] += value.reshape(ref.shape[1:])

    def make_message(t, u):
        for part in range(2):
            span = pl.ds(part * count, count)
            block = to_slots(slots, feat, u * width + part * count, count)
            feat_slot[u, span, :] = block
            pre = dot(block, wr[...])
            out[u, span, :] = (pre * jax.nn.sigmoid(pre)).astype(jnp.bfloat16)

        @pl.when(t == 1)
        def _():
            for off in range(1, ZN):
                key_copy(off).wait_recv()

    def coarse_update(span, total):
        summed = coarse[span, :].astype(jnp.float32) + total
        rounded = summed.astype(jnp.bfloat16)
        moved = dot(rounded, wc[...])
        summed_b[span, :] = rounded
        update[span, :] = moved
        chunks[0, span, :] = (summed + moved * jax.nn.sigmoid(moved)).astype(jnp.bfloat16)

    rows_a = Rows(here, out, into_a, pass_ra, pass_la, x_send_a, x_recv_a)
    sum_to_owners(here, rows_a, make_message, keys, coarse_update, out_z, got, z_send_a, z_recv_a)
    for off in range(1, ZN):
        key_copy(off).wait_send()

    def place_cotangent(i):
        @pl.when(i < ZN)
        def _():
            u = here.plane(cast_off(i))
            for part in range(2):
                span = pl.ds(part * count, count)
                cot_slot[u, span, :] = to_slots(slots, cot, u * width + part * count, count)

    def new_places(u, first, count):
        found = turned(keys[u, :, first:first + count]).astype(jnp.int16)
        key_places[u, first:first + count, :] = found
        return found

    def old_places(u, first, count):
        return key_places[u, first:first + count, :]

    def make_term(t, u):
        for part in range(2):
            span = pl.ds(part * count, count)
            parent = into_b[u, span, :]
            proj = dot(parent, wp[...])
            grad = (cot_slot[u, span, :].astype(jnp.float32) * dsilu(proj)).astype(jnp.bfloat16)
            add(part_cp, 1, left_dot(parent, grad))
            term[u, span, :] = right_dot(grad, wp[...]).astype(jnp.bfloat16)

        @pl.when(t == 2)
        def _():
            back[...] = jnp.zeros_like(back)
            for at in range(0, nodes, step):
                places[at:at + step, :] = turned(slots[:, at:at + step]).astype(jnp.int16)

    rows_b = Rows(here, out, into_b, pass_rb, pass_lb, x_send_b, x_recv_b)
    cast_to_children(
        here, rows_b, new_places, place_cotangent, lambda t, u: None, chunks, z_send_b, z_recv_b
    )

    def coarse_gradient(span, total):
        grad_update = (total * dsilu(update[span, :])).astype(jnp.bfloat16)
        grad = (total + right_dot(grad_update, wc[...])).astype(jnp.bfloat16)
        grad_coarse[span, :] = grad
        chunks[0, span, :] = grad
        add(part_cp, 0, left_dot(summed_b[span, :], grad_update))

    rows_a = Rows(here, term, into_a, pass_ra, pass_la, x_send_a, x_recv_a)
    sum_to_owners(
        here, rows_a, make_term, keys, coarse_gradient, out_z, got, z_send_a, z_recv_a
    )

    sums_cp = Total(here, part_cp, scale, *total_refs[:8], total_refs[16])
    sums_r = Total(here, part_r, scale, *total_refs[8:16], total_refs[17])

    def other_sums(i):
        for stage in range(6):
            pl.when(i == stage)(functools.partial(sums_cp.next, stage))

    def node_gradient(t, u):
        for part in range(2):
            span = pl.ds(part * count, count)
            block = feat_slot[u, span, :]
            pre = dot(block, wr[...])
            grad = (into_b[u, span, :].astype(jnp.float32) * dsilu(pre)).astype(jnp.bfloat16)
            add(part_r, 0, left_dot(block, grad))
            grad_pre[span, :] = grad

        pl.when(t == ZN - 1)(functools.partial(sums_r.next, 0))
        first = jnp.full((step, places.shape[1]), u * width, jnp.int32).astype(jnp.int16)

        @pl.loop(0, nodes // step, unroll=2)
        def _(part):
            span = pl.ds(pl.multiple_of(part * step, step), step)
            wanted = places[span, :] - first
            found = dot(columns_hot(wanted, width), grad_pre[...])
            back[span, :] = (back[span, :].astype(jnp.float32) + found).astype(jnp.bfloat16)

    rows_b = Rows(here, out, into_b, pass_rb, pass_lb, x_send_b, x_recv_b)
    cast_to_children(here, rows_b, old_places, other_sums, node_gradient, chunks, z_send_b, z_recv_b)
    sums_r.next(1)

    @pl.loop(0, nodes // step)
    def _(part):
        span = pl.ds(pl.multiple_of(part * step, step), step)
        grad_node[span, :] = (
            cot[span, :].astype(jnp.float32) + right_dot(back[span, :], wr[...])
        ).astype(jnp.bfloat16)

    for stage in range(2, 6):
        sums_r.next(stage)
    total_r[...] = sums_r.full[0].reshape(total_r.shape)
    total_c[...] = sums_cp.full[0].reshape(total_c.shape)
    total_p[...] = sums_cp.full[1].reshape(total_p.shape)


def total_scratch(m, groups, width):
    rows = width // groups
    part = rows // XN
    return [
        pltpu.VMEM((m, groups, rows, width), jnp.float32),
        pltpu.VMEM((m, XN, part, width), jnp.float32),
        pltpu.VMEM((m, XN, part, width), jnp.float32),
        pltpu.VMEM((m, part, width), jnp.float32),
        pltpu.VMEM((ZN, m, part, width), jnp.float32),
        pltpu.VMEM((m, part, width), jnp.float32),
        pltpu.VMEM((m, XN, part, width), jnp.float32),
        pltpu.VMEM((m, groups, XN, part, width), jnp.float32),
    ]


def local(
    node_feat, coarse_feat, cotangent, w_restrict, w_coarse, w_prolong, owner, slot, recv_row
):
    devs = ZN * XN
    groups = lax.axis_size("grp")
    nodes, width = node_feat.shape
    coarse_rows = coarse_feat.shape[0]
    block = recv_row.shape[0] // devs
    plane_rows = XN * block
    bf, f32 = jnp.bfloat16, jnp.float32
    shape = jax.ShapeDtypeStruct
    dma = pltpu.SemaphoreType.DMA
    vmem = pltpu.VMEM
    wide = vmem((ZN, plane_rows, width), bf)
    passing = vmem((ZN, block // 2, width), bf)
    scratch = [
        vmem((ZN, 1, plane_rows), jnp.int32),
        wide,
        wide,
        wide,
        wide,
        vmem((coarse_rows, width), bf),
        vmem((coarse_rows, width), f32),
        vmem((ZN, plane_rows, 128), jnp.int16),
        vmem((nodes, 128), jnp.int16),
        vmem((plane_rows, width), bf),
        vmem((nodes, width), bf),
        wide, passing, passing,
        wide, passing, passing,
        vmem((ZN, coarse_rows, width), bf),
        vmem((ZN + 1, coarse_rows, width), bf),
        vmem((ZN, coarse_rows, width), bf),
    ]
    scratch += [dma((6, ZN))] * 4 + [dma((ZN,)), dma((ZN + 1,))] * 2 + [dma((ZN,))] * 2
    scratch += [
        vmem((2, groups, width // groups, width), f32),
        vmem((1, groups, width // groups, width), f32),
    ]
    scratch += total_scratch(2, groups, width) + total_scratch(1, groups, width)
    scratch += [dma((2, 5, ZN))] * 2
    in_vmem = pl.BlockSpec(memory_space=pltpu.VMEM)
    scale = float(nodes * devs * groups) ** (-0.5)
    weight = shape((width, width), f32)
    return pl.pallas_call(
        functools.partial(block_kernel, scale),
        out_shape=(
            shape((nodes, width), bf),
            shape((coarse_rows, width), bf),
            weight, weight, weight,
        ),
        in_specs=[in_vmem] * 8,
        out_specs=(in_vmem,) * 5,
        scratch_shapes=scratch,
        compiler_params=pltpu.CompilerParams(
            collective_id=0, has_side_effects=True, vmem_limit_bytes=62 * 2**20
        ),
    )(
        node_feat, cotangent, (owner * block + slot).reshape(1, nodes),
        recv_row.reshape(ZN, 1, plane_rows), coarse_feat, w_restrict, w_coarse, w_prolong,
    )

def solution(mesh):
    return jax.shard_map(
        local,
        mesh=mesh,
        in_specs=(
            P(("grp", "dev"), None),
            P(("grp", "dev"), None),
            P(("grp", "dev"), None),
            P(),
            P(),
            P(),
            P(("grp", "dev")),
            P(("grp", "dev")),
            P(("grp", "dev")),
        ),
        out_specs=(P(("grp", "dev"), None), P(("grp", "dev"), None), P(), P(), P()),
        check_vma=False,
    )
```
